32 devices in a mesh: dp: 8 (over y, x, core), tensor: 4 (over z).
Axes of the slice: x: 2, y: 2, z: 4, core: 2. Of those that a mesh axis runs over, the one named last changes fastest.
Arguments:
- inputs: bfloat16 [2048, 4096], P('dp', 'tensor'), may hold values from -6 to 6
- first_factor: bfloat16 [256, 16, 1024], P(None, 'tensor'), may hold values from -0.375 to 0.375
- second_factor: bfloat16 [1024, 16, 1024], P(None, 'tensor'), may hold values from -0.1875 to 0.1875
- cotangent: bfloat16 [16384, 2048], P('tensor', 'dp'), may hold values from -6 to 6
Outputs:
- input_grad: bfloat16 [2048, 4096], P('dp', 'tensor')
- first_grad: float32 [256, 16, 1024], P('dp', 'tensor')
The draws below stay inside these ranges and needn't reach their ends.
All inputs are finite; a program needn't handle non-finite values.
Results may differ from the reference program's by a relative error of at most 0.0063.
Values may be sent and summed in bfloat16 or wider, within the bound.
No kernel may reach another device: no remote copies, remote signals or barrier semaphores. Data moves between devices by JAX's collectives and lax.ppermute only.
A program may use at most 64 MiB of HBM per device.

```python
import jax
import jax.numpy as jnp
from jax import lax

MODEL_WIDTH = 4096
HIDDEN_SIZE = 16384
BLOCKS = 16
TOK_DEV = 256
TOKENS = 2048
IN_BLK = 256
OUT_BLK = 1024
GROUP = 64
N_DP = 8


def block_scale(key, dims, shards, least, high):
    gain, own = 1.0, jax.random.fold_in(key, 6)
    for dim, parts in shards:
        steps = jnp.exp(jax.random.uniform(jax.random.fold_in(own, dim), (parts,), jnp.float32, least / len(shards), high / len(shards)))
        gain = gain * jnp.repeat(steps, dims[dim] // parts).reshape([-1 if axis == dim else 1 for axis in range(len(dims))])
    return gain


def gaussian(key, shape, width, limit, split=(), held_as=jnp.bfloat16):
    drawn = width * jax.random.normal(key, shape, jnp.float32)
    if split:
        drawn = drawn * block_scale(key, shape, split, -0.22, 0.18)
    return jnp.clip(drawn, -limit, limit).astype(held_as)


def setup_inputs(seed: int = 0) -> dict:
    key_list = jax.random.split(jax.random.key(seed), 5)
    return {
        "inputs": gaussian(key_list[0], (TOKENS, MODEL_WIDTH), 1.0, 6.0, ((0, 8), (1, 4))),
        "first_factor": gaussian(key_list[1], (IN_BLK, BLOCKS, OUT_BLK), IN_BLK ** -0.5, 0.375, ((1, 4),)),
        "second_factor": gaussian(key_list[2], (OUT_BLK, BLOCKS, OUT_BLK), OUT_BLK ** -0.5, 0.1875, ((1, 4),)),
        "cotangent": gaussian(key_list[3], (HIDDEN_SIZE, TOKENS), 1.0, 6.0, ((0, 4), (1, 8))),
    }


def gelu_backward(pre_act, upstream):
    value, pullback = jax.vjp(lambda v: jax.nn.gelu(v, approximate=True), pre_act)
    return pullback(upstream)[0]

def rounded_activation(value):
    return lax.optimization_barrier(value.astype(jnp.bfloat16)).astype(jnp.float32)

def reference(inputs, first_factor, second_factor, cotangent):
    initial_expanded = first_factor.astype(jnp.float32)
    second_wide = second_factor.astype(jnp.float32)

    def tile_step(carry, tile):
        leading_gradient = carry
        inputs_tile, cot_tile = tile
        row_count = inputs_tile.shape[0]
        block_grouped = inputs_tile.reshape(row_count, BLOCKS, IN_BLK).astype(jnp.float32)
        initial_output = rounded_activation(jnp.einsum('rvh,hva->rva', block_grouped, initial_expanded))
        mixed = initial_output.reshape(row_count, BLOCKS, BLOCKS, GROUP).transpose(0, 2, 1, 3).reshape(row_count, BLOCKS, OUT_BLK)
        pre_act = jnp.einsum('tjm,mjn->jnt', mixed, second_wide)
        upstream = cot_tile.reshape(BLOCKS, OUT_BLK, row_count).astype(jnp.float32)
        pre_grad = rounded_activation(gelu_backward(pre_act, upstream))
        mixed_grad = rounded_activation(jnp.einsum('jnt,mjn->tjm', pre_grad, second_wide))
        output_gradient = mixed_grad.reshape(row_count, BLOCKS, BLOCKS, GROUP).transpose(0, 2, 1, 3).reshape(row_count, BLOCKS, OUT_BLK)
        leading_gradient = leading_gradient + jnp.einsum('cvq,cvs->qvs', block_grouped, output_gradient)
        input_slab = jnp.einsum('ius,yus->iuy', output_gradient, initial_expanded).reshape(row_count, MODEL_WIDTH).astype(jnp.bfloat16)
        return (leading_gradient, input_slab)
    start_one = jnp.zeros((IN_BLK, BLOCKS, OUT_BLK), jnp.float32)
    tiles_in = inputs.reshape(N_DP, TOK_DEV, MODEL_WIDTH)
    tiles_cot = cotangent.reshape(HIDDEN_SIZE, N_DP, TOK_DEV).transpose(1, 0, 2)
    leading_gradient, input_tiles = lax.scan(tile_step, start_one, (tiles_in, tiles_cot))
    factor = jnp.float32(TOKENS ** (-0.5))
    return (input_tiles.reshape(TOKENS, MODEL_WIDTH), leading_gradient * factor)
```

```python
import functools

import jax
import jax.numpy as jnp
from jax import lax
from jax.experimental import pallas as pl
from jax.experimental.pallas import tpu as pltpu
from jax.sharding import PartitionSpec as P

BF16 = jnp.bfloat16
F32 = jnp.float32


def dot(a, b, dims):
    return lax.dot_general(a, b, (dims, ((), ())), preferred_element_type=F32)


def gelu_slope(v):
    c = 0.7978845608028654
    v2 = v * v
    t = jnp.tanh(v * (c + (c * 0.044715) * v2))
    return 0.5 + 0.5 * t + (0.5 * v) * (1.0 - t * t) * (c + (3.0 * c * 0.044715) * v2)


VMEM = pl.BlockSpec(memory_space=pltpu.VMEM)
SMALL = pltpu.CompilerParams(vmem_limit_bytes=16 << 20)
FREE = pl.CostEstimate(flops=0, bytes_accessed=0, transcendentals=0)
SMEM = pl.BlockSpec(memory_space=pltpu.SMEM)


def on_chip(kernel, name, at, operands, shapes, stored=(), limit=16 << 20, **more):
    held = [pltpu.with_memory_space_constraint(a, pltpu.VMEM) for a in operands]
    out = [pltpu.VMEM(shape, dtype) for shape, dtype in shapes]
    return pl.pallas_call(
        kernel,
        in_specs=[SMEM] + [VMEM] * len(held) + [pl.BlockSpec(memory_space=pl.ANY)] * len(stored),
        out_specs=[VMEM] * len(out),
        out_shape=out,
        compiler_params=pltpu.CompilerParams(vmem_limit_bytes=limit),
        cost_estimate=FREE,
        name=name,
        **more,
    )(at, *held, *stored)


def cut_kernel(nz, local, cols, kd, at_ref, f_ref, *outs):
    for r in range(1, nz):
        col = pl.multiple_of(lax.rem(at_ref[0] + nz - r, nz) * cols, cols)
        for b in range(local):
            outs[r - 1][b] = f_ref[:, b, pl.ds(col, cols)]


def cut(at, first_factor, nz, nd):
    width, local, out_width = first_factor.shape
    kd, cols = width // nd, out_width // nz
    return pl.pallas_call(
        functools.partial(cut_kernel, nz, local, cols, kd),
        grid_spec=pltpu.PrefetchScalarGridSpec(
            num_scalar_prefetch=1,
            grid=(1,),
            in_specs=[pl.BlockSpec((kd, local, out_width), lambda i, at_ref: (at_ref[1], 0, 0))],
            out_specs=[pl.BlockSpec((local, kd, cols), lambda i, at_ref: (0, 0, 0))] * (nz - 1),
        ),
        out_shape=[pltpu.VMEM((local, kd, cols), BF16)] * (nz - 1),
        compiler_params=SMALL,
        cost_estimate=FREE,
        name="cut",
    )(at, first_factor)


def own_kernel(local, at_ref, f_ref, later_ref, out):
    for b in range(local):
        out[b] = f_ref[:, b, :]


def own_columns(at, first_factor, earlier, nz):
    width, local, out_width = first_factor.shape
    cols = out_width // nz
    return pl.pallas_call(
        functools.partial(own_kernel, local),
        grid_spec=pltpu.PrefetchScalarGridSpec(
            num_scalar_prefetch=1,
            grid=(1,),
            in_specs=[pl.BlockSpec((width, local, cols), lambda i, at_ref: (0, 0, at_ref[0])), VMEM],
            out_specs=pl.BlockSpec((local, width, cols), lambda i, at_ref: (0, 0, 0)),
        ),
        out_shape=pltpu.VMEM((local, width, cols), BF16),
        compiler_params=SMALL,
        cost_estimate=FREE,
        name="own_columns",
    )(at, first_factor, pltpu.with_memory_space_constraint(earlier, pltpu.VMEM))


def turn_kernel(x_ref, later_ref, out):
    out[...] = x_ref[...].T


def turned(cotangent, earlier, tile=512):
    units, tokens = cotangent.shape
    return pl.pallas_call(
        turn_kernel,
        grid=(units // tile,),
        in_specs=[pl.BlockSpec((tile, tokens), lambda i: (i, 0)), VMEM],
        out_specs=pl.BlockSpec((tokens, tile), lambda i: (0, i)),
        out_shape=pltpu.VMEM((tokens, units), BF16),
        compiler_params=SMALL,
        cost_estimate=FREE,
        name="turned",
    )(cotangent, pltpu.with_memory_space_constraint(earlier, pltpu.VMEM))


def assemble_kernel(local, kd, orders, at_ref, own_ref, *refs):
    out = refs[-1]
    out[:local] = own_ref[...]
    core = jnp.bitwise_and(at_ref[1], 1)
    at = local
    for i, order in enumerate(orders):
        mine, other = refs[2 * i], refs[2 * i + 1]
        bits = len(order) + 1
        blocks = mine.shape[bits - 1]
        for d in range(1 << bits):
            place = tuple((d >> bit) & 1 for bit in reversed(order))
            for b in range(blocks):
                rows = jnp.where(core == (d & 1), mine[place + (b,)], other[place + (b,)])
                out[at + b, d * kd : (d + 1) * kd, :] = rows
        at += blocks


def layer_kernel(nz, local, width, cols, chunk, at_ref, *refs):
    x_refs = refs[:nz]
    f_ref, cot_ref = refs[nz : nz + 2]
    s_hbm, *dx_refs, og_ref, mixed, back, s_ref, arrived = refs[-(nz + 6) :]
    fetch = [pltpu.make_async_copy(s_hbm.at[j], s_ref.at[j], arrived.at[j]) for j in range(local)]
    for copy in fetch:
        copy.start()
    z = at_ref[0]
    group = cols // local
    rows, out_width = dx_refs[0].shape[0], mixed.shape[2]
    here = slice(chunk * rows, (chunk + 1) * rows)
    low = lax.broadcasted_iota(jnp.int32, (rows, 2 * group), 1) < group

    for r in range(nz):
        for b in range(0, local, 2):
            one = dot(x_refs[r][:, b * width : (b + 1) * width], f_ref[r * local + b], ((1,), (0,)))
            two = dot(x_refs[r][:, (b + 1) * width : (b + 2) * width], f_ref[r * local + b + 1], ((1,), (0,)))
            at = (r * local + b) * group
            for h in range(local // 2):
                p = one[:, 2 * h * group : (2 * h + 2) * group]
                q = two[:, 2 * h * group : (2 * h + 2) * group]
                mixed[2 * h, :, at : at + 2 * group] = jnp.where(low, p, pltpu.roll(q, group, 1)).astype(BF16)
                mixed[2 * h + 1, :, at : at + 2 * group] = jnp.where(low, pltpu.roll(p, group, 1), q).astype(BF16)

    planes = [lax.rem(z + r, nz) for r in range(nz)]

    for j in range(local):
        fetch[j].wait()
        weight = jnp.concatenate(
            [s_ref[j, pl.ds(pl.multiple_of(p * cols, cols), cols), :] for p in planes], axis=0
        )
        pre_act = dot(mixed[j], weight, ((1,), (0,)))
        upstream = cot_ref[here, j * out_width : (j + 1) * out_width]
        pre_grad = (upstream.astype(F32) * gelu_slope(pre_act)).astype(BF16)
        back[j] = dot(pre_grad, weight, ((1,), (1,)))

    for r in range(nz):
        for b in range(0, local, 2):
            at = (r * local + b) * group
            one, two = [], []
            for h in range(local // 2):
                p = back[2 * h, :, at : at + 2 * group]
                q = back[2 * h + 1, :, at : at + 2 * group]
                one.append(jnp.where(low, p, pltpu.roll(q, group, 1)).astype(BF16))
                two.append(jnp.where(low, pltpu.roll(p, group, 1), q).astype(BF16))
            for i, part in ((b, one), (b + 1, two)):
                og = jnp.concatenate(part, axis=1)
                og_ref[r, :, i * cols : (i + 1) * cols] = og
                dx_refs[r][:, i * width : (i + 1) * width] = dot(
                    og, f_ref[r * local + i], ((1,), (1,))
                ).astype(dx_refs[r].dtype)


def layer(at, xs, first, second, cot, later, chunk, rows, nz, local, width, cols):
    out_width = second.shape[2]
    piece = (rows, local * width)
    return on_chip(
        functools.partial(layer_kernel, nz, local, width, cols, chunk),
        "layer",
        at,
        list(xs) + [first, cot, *later],
        [(piece, F32)] + [(piece, BF16)] * (nz - 1) + [((nz, rows, local * cols), BF16)],
        scratch_shapes=[
            pltpu.VMEM((local, rows, out_width), BF16),
            pltpu.VMEM((local, rows, out_width), F32),
            pltpu.VMEM(second.shape, BF16),
            pltpu.SemaphoreType.DMA((local,)),
        ],
        stored=[second],
        limit=28 << 20,
    )


def grad_kernel(nz, parts, local, width, cols, nd, at_ref, *refs):
    x_refs, og_refs = refs[: parts * nz], refs[parts * nz : parts * (nz + 1)]
    give, keep = refs[-2:]
    me = at_ref[1]
    kd = width // nd
    for r in range(nz):
        for b in range(local):
            x = jnp.concatenate(
                [x_refs[c * nz + r][:, b * width : (b + 1) * width] for c in range(parts)], axis=0
            )
            og = jnp.concatenate([og_refs[c][r, :, b * cols : (b + 1) * cols] for c in range(parts)], axis=0)
            term = dot(x, og, ((0,), (0,))).astype(BF16)
            for d in range(0, nd, 2):
                to = lax.div(jnp.bitwise_xor(me, d), 2)
                low, high = term[d * kd : (d + 1) * kd], term[(d + 1) * kd : (d + 2) * kd]
                odd = jnp.bitwise_and(me, 1) == 1
                keep[to, r * local + b] = jnp.where(odd, high, low)
                give[to, r * local + b] = jnp.where(odd, low, high)


def first_grad_terms(at, xs, ogs, later, nz, local, width, cols, nd):
    shape = (nd // 2, nz * local, width // nd, cols)
    return on_chip(
        functools.partial(grad_kernel, nz, len(ogs), local, width, cols, nd),
        "first_grad_terms",
        at,
        [a for x in xs for a in x] + list(ogs) + list(later),
        [(shape, BF16)] * 2,
    )


def sums_kernel(plan, at_ref, *refs):
    used = 0
    for i, has_got in enumerate(plan):
        total = refs[used][...]
        if has_got:
            total = (total.astype(F32) + refs[used + 1][...].astype(F32)).astype(BF16)
        used += 1 + has_got
        refs[i - len(plan)][...] = total


def sums(at, pairs, *earlier):
    return on_chip(
        functools.partial(sums_kernel, [got is not None for _, got in pairs]),
        "sums",
        at,
        [a for pair in pairs for a in pair if a is not None] + list(earlier),
        [(part.shape, BF16) for part, _ in pairs],
    )


def after(at, values, *earlier):
    return on_chip(
        functools.partial(sums_kernel, [False] * len(values)),
        "after",
        at,
        list(values) + list(earlier),
        [(v.shape, v.dtype) for v in values],
    )


def halved_kernel(count, at_ref, *refs):
    low, high = refs[-2:]
    half, size = low.shape[0], refs[0].shape[0]
    for i in range(count):
        for b in range(size):
            at = i * size + b
            (low if at < half else high)[at % half] = refs[i][b]


def halved(at, blocks, *earlier):
    size, kd, cols = blocks[0].shape
    shape = (len(blocks) * size // 2, kd, cols)
    return on_chip(
        functools.partial(halved_kernel, len(blocks)), "halved", at, list(blocks) + list(earlier), [(shape, BF16)] * 2
    )


def join_kernel(count, at_ref, *refs):
    out = refs[-1]
    rows = refs[0].shape[0]
    for c in range(count):
        out[c * rows : (c + 1) * rows] = (refs[2 * c][...] + refs[2 * c + 1][...].astype(F32)).astype(BF16)


def join(at, pairs):
    held = [pltpu.with_memory_space_constraint(a, pltpu.VMEM) for pair in pairs for a in pair]
    rows, width = held[0].shape
    return pl.pallas_call(
        functools.partial(join_kernel, len(pairs)),
        in_specs=[SMEM] + [VMEM] * len(held),
        out_specs=VMEM,
        out_shape=jax.ShapeDtypeStruct((rows * len(pairs), width), BF16),
        compiler_params=SMALL,
        cost_estimate=FREE,
        name="join",
    )(at, *held)


def place_kernel(nz, local, cols, factor, at_ref, *refs):
    out = refs[-1]
    for r in range(nz):
        at = pl.multiple_of(lax.rem(at_ref[0] + nz - r, nz) * cols, cols)
        for b in range(local):
            out[:, b, pl.ds(at, cols)] = refs[r][b].astype(F32) * factor


def place(at, pieces, factor):
    nz = len(pieces)
    local, kd, cols = pieces[0].shape
    held = [pltpu.with_memory_space_constraint(a, pltpu.VMEM) for a in pieces]
    return pl.pallas_call(
        functools.partial(place_kernel, nz, local, cols, factor),
        in_specs=[SMEM] + [VMEM] * nz,
        out_specs=VMEM,
        out_shape=jax.ShapeDtypeStruct((kd, local, nz * cols), F32),
        compiler_params=SMALL,
        cost_estimate=FREE,
        name="place",
    )(at, *held)


def swap(bit, nd):
    return [(i, i ^ (1 << bit)) for i in range(nd)]


def ring_step(value, step, nz):
    return lax.ppermute(value, "tensor", [(i, (i + step) % nz) for i in range(nz)])


def double_over_dp(part, bit, d, nd):
    got = lax.ppermute(part, "dp", swap(bit, nd))
    upper = (d >> bit) & 1 == 1
    return jnp.stack([jnp.where(upper, got, part), jnp.where(upper, part, got)])


def body(inputs, first_factor, second_factor, cotangent):
    nz, nd = lax.axis_size("tensor"), lax.axis_size("dp")
    z, d = lax.axis_index("tensor"), lax.axis_index("dp")
    at = jnp.stack([z, d]).astype(jnp.int32)
    tokens_here = inputs.shape[0]
    width, local, out_width = first_factor.shape
    cols = out_width // nz
    kd = width // nd
    steps = (1, -1)
    rows = tokens_here // len(steps)
    bits = nd.bit_length() - 1
    orders = [list(range(1, bits)), list(range(bits - 1, 0, -1))]

    turn = lambda c, n: (-n * steps[c]) % nz
    xs = [[inputs[c * rows : (c + 1) * rows]] + [None] * (nz - 1) for c in range(len(steps))]
    for c in range(len(steps)):
        xs[c][turn(c, 1)] = ring_step(xs[c][0], steps[c], nz)

    def pass_on(n, *earlier, also=()):
        came = after(at, [xs[c][turn(c, n - 1)] for c in range(len(steps))] + list(also), *earlier)
        for c in range(len(steps)):
            xs[c][turn(c, n - 1)] = came[c]
            xs[c][turn(c, n)] = ring_step(came[c], steps[c], nz)
        return came[len(steps) :]

    second = second_factor.transpose(1, 0, 2)
    sends = cut(at, first_factor, nz, nd)
    got = [ring_step(sends[r - 1], -r, nz) for r in range(1, nz)]
    if nz > 2:
        pass_on(2, *got)
    others = halved(at, got, *[xs[c][turn(c, 1)] for c in range(len(steps))])
    for k in range(max(bits - 1, 1)):
        if bits > 1:
            others = [double_over_dp(o, order[k], d, nd) for o, order in zip(others, orders)]
        if k == 0:
            cot = turned(cotangent, others[0])
            own = own_columns(at, first_factor, others[1], nz)
    if nz > 3:
        others = pass_on(3, own, cot, also=others)
    for n in range(4, nz):
        pass_on(n)
    pieces = []
    for o in others:
        pieces += [o, lax.ppermute(o, "dp", swap(0, nd))]
    first = on_chip(
        functools.partial(assemble_kernel, local, kd, orders),
        "assemble",
        at,
        [own] + pieces,
        [((nz * local, width, cols), BF16)],
    )[0]

    parts, ogs = [], []
    for c in range(len(steps)):
        later = [xs[1][turn(1, nz - 1)]] if c == 0 else []
        res = layer(at, xs[c], first, second, cot, later, c, rows, nz, local, width, cols)
        parts.append(res[:nz])
        ogs.append(res[nz])
    ring = [ring_step(parts[0][turn(0, 1)], steps[0], nz), None]

    def ring_next(n, *earlier):
        pairs, whose = [], []
        if n < nz:
            pairs.append((parts[0][turn(0, n)], ring[0]))
            whose.append(0)
        pairs.append((parts[1][turn(1, n - 1)], ring[1]))
        whose.append(1)
        sent = sums(at, pairs, *earlier)
        for c, send in zip(whose, sent):
            ring[c] = ring_step(send, steps[c], nz)
        return sent

    sent = ring_next(2)
    give, keep = first_grad_terms(at, xs, ogs, sent, nz, local, width, cols, nd)
    got = lax.ppermute(give, "dp", swap(0, nd))
    keep = keep.reshape([2] * (bits - 1) + list(keep.shape[1:]))
    got = got.reshape(keep.shape)
    half = nz * local // 2
    totals = []
    for i in range(2):
        cut_half = lambda a: a[(slice(None),) * (bits - 1) + (slice(i * half, (i + 1) * half),)]
        totals.append(cut_half(keep).astype(F32) + cut_half(got).astype(F32))
    left = [list(range(bits - 1, 0, -1)) for _ in range(2)]
    for k in range(bits - 1):
        give = []
        for i in range(2):
            axis = left[i].index(orders[i][k])
            left[i].remove(orders[i][k])
            pick = lambda n: lax.index_in_dim(totals[i], n, axis, keepdims=False)
            give.append(pick(1).astype(BF16))
            totals[i] = pick(0)
        if k == 0 and nz > 2:
            ring_next(3, *give)
        for i in range(2):
            totals[i] = totals[i] + lax.ppermute(give[i], "dp", swap(orders[i][k], nd)).astype(F32)
    blocks = jnp.concatenate(totals, axis=0).reshape(nz, local, kd, cols)
    give = [blocks[r].astype(BF16) for r in range(1, nz)]
    pieces = [blocks[0]] + [ring_step(give[r - 1], r, nz) for r in range(1, nz)]
    for n in range(4, nz + 1):
        ring_next(n, *pieces[1:], ring[0])
    first_sum = place(at, pieces, (tokens_here * nd) ** (-0.5))
    return join(at, [(parts[c][0], ring[c]) for c in range(len(steps))]), first_sum


def plain_body(inputs, first_factor, second_factor, cotangent):
    tokens_here = inputs.shape[0]
    in_width, local, out_width = first_factor.shape
    blocks = local * lax.axis_size("tensor")
    group = out_width // blocks
    block_grouped = inputs.reshape(tokens_here, local, in_width)
    split_first = first_factor.reshape(in_width, local, blocks, group)
    outgoing = jnp.einsum("tlk,kljg->jlgt", block_grouped, split_first, preferred_element_type=F32).astype(BF16)
    arrived = lax.all_to_all(outgoing, "tensor", split_axis=0, concat_axis=1, tiled=True)
    mixed = arrived.reshape(local, out_width, tokens_here)
    pre_act = jnp.einsum("lmt,mln->lnt", mixed, second_factor, preferred_element_type=F32)
    upstream = cotangent.reshape(local, out_width, tokens_here).astype(F32)
    pre_grad = (upstream * gelu_slope(pre_act)).astype(BF16)
    mixed_grad = jnp.einsum("lnt,mln->lmt", pre_grad, second_factor, preferred_element_type=F32).astype(BF16)
    returned = lax.all_to_all(
        mixed_grad.reshape(local, blocks, group, tokens_here), "tensor", split_axis=1, concat_axis=0, tiled=True
    )
    input_grad = jnp.einsum("jlgt,kljg->tlk", returned, split_first, preferred_element_type=F32)
    input_grad = input_grad.reshape(tokens_here, local * in_width).astype(BF16)
    factor = (tokens_here * lax.axis_size("dp")) ** (-0.5)
    first_term = jnp.einsum("tlk,jlgt->kljg", block_grouped, returned, preferred_element_type=F32)
    first_term = first_term.reshape(in_width, local, out_width)
    first_sum = lax.psum_scatter(first_term, "dp", scatter_dimension=0, tiled=True)
    return input_grad, first_sum * factor


def solution(mesh):
    nz, nd = mesh.shape["tensor"], mesh.shape["dp"]

    def run(inputs, first_factor, second_factor, cotangent):
        width, local, _ = first_factor.shape
        fits = local % 2 == 0 and width % (16 * nd) == 0 and nd & (nd - 1) == 0
        return (body if fits else plain_body)(inputs, first_factor, second_factor, cotangent)

    return jax.shard_map(
        run,
        mesh=mesh,
        in_specs=(
            P("dp", "tensor"),
            P(None, "tensor", None),
            P(None, "tensor", None),
            P("tensor", "dp"),
        ),
        out_specs=(P("dp", "tensor"), P("dp", "tensor", None)),
        check_vma=False,
    )
```

```python
import functools

import jax
import jax.numpy as jnp
from jax import lax
from jax.experimental import pallas as pl
from jax.experimental.pallas import tpu as pltpu
from jax.sharding import PartitionSpec as P

BF16 = jnp.bfloat16
F32 = jnp.float32


def dot(a, b, dims):
    return lax.dot_general(a, b, (dims, ((), ())), preferred_element_type=F32)


def gelu_slope(v):
    c = 0.7978845608028654
    v2 = v * v
    t = jnp.tanh(v * (c + (c * 0.044715) * v2))
    return 0.5 + 0.5 * t + (0.5 * v) * (1.0 - t * t) * (c + (3.0 * c * 0.044715) * v2)


VMEM = pl.BlockSpec(memory_space=pltpu.VMEM)
SMALL = pltpu.CompilerParams(vmem_limit_bytes=16 << 20)
FREE = pl.CostEstimate(flops=0, bytes_accessed=0, transcendentals=0)
SMEM = pl.BlockSpec(memory_space=pltpu.SMEM)


def on_chip(kernel, name, at, operands, shapes, stored=(), limit=16 << 20, **more):
    held = [pltpu.with_memory_space_constraint(a, pltpu.VMEM) for a in operands]
    held += [pltpu.with_memory_space_constraint(a, pltpu.HBM) for a in stored]
    out = [pltpu.VMEM(shape, dtype) for shape, dtype in shapes]
    return pl.pallas_call(
        kernel,
        in_specs=[SMEM] + [VMEM] * len(operands) + [pl.BlockSpec(memory_space=pltpu.HBM)] * len(stored),
        out_specs=[VMEM] * len(out),
        out_shape=out,
        compiler_params=pltpu.CompilerParams(vmem_limit_bytes=limit),
        cost_estimate=FREE,
        name=name,
        **more,
    )(at, *held)


def cut_kernel(nz, local, cols, kd, at_ref, f_ref, *outs):
    for r in range(1, nz):
        col = pl.multiple_of(lax.rem(at_ref[0] + nz - r, nz) * cols, cols)
        for b in range(local):
            outs[r - 1][b] = f_ref[:, b, pl.ds(col, cols)]


def cut(at, first_factor, nz, nd):
    width, local, out_width = first_factor.shape
    kd, cols = width // nd, out_width // nz
    return pl.pallas_call(
        functools.partial(cut_kernel, nz, local, cols, kd),
        grid_spec=pltpu.PrefetchScalarGridSpec(
            num_scalar_prefetch=1,
            grid=(1,),
            in_specs=[pl.BlockSpec((kd, local, out_width), lambda i, at_ref: (at_ref[1], 0, 0))],
            out_specs=[pl.BlockSpec((local, kd, cols), lambda i, at_ref: (0, 0, 0))] * (nz - 1),
        ),
        out_shape=[pltpu.VMEM((local, kd, cols), BF16)] * (nz - 1),
        compiler_params=SMALL,
        cost_estimate=FREE,
        name="cut",
    )(at, first_factor)


def own_kernel(local, at_ref, f_ref, later_ref, out):
    for b in range(local):
        out[b] = f_ref[:, b, :]


def own_columns(at, first_factor, earlier, nz):
    width, local, out_width = first_factor.shape
    cols = out_width // nz
    return pl.pallas_call(
        functools.partial(own_kernel, local),
        grid_spec=pltpu.PrefetchScalarGridSpec(
            num_scalar_prefetch=1,
            grid=(1,),
            in_specs=[pl.BlockSpec((width, local, cols), lambda i, at_ref: (0, 0, at_ref[0])), VMEM],
            out_specs=pl.BlockSpec((local, width, cols), lambda i, at_ref: (0, 0, 0)),
        ),
        out_shape=pltpu.VMEM((local, width, cols), BF16),
        compiler_params=SMALL,
        cost_estimate=FREE,
        name="own_columns",
    )(at, first_factor, pltpu.with_memory_space_constraint(earlier, pltpu.VMEM))


def turn_kernel(x_ref, later_ref, out):
    out[...] = x_ref[...].T


def turned(cotangent, earlier, tile=512):
    units, tokens = cotangent.shape
    return pl.pallas_call(
        turn_kernel,
        grid=(units // tile,),
        in_specs=[pl.BlockSpec((tile, tokens), lambda i: (i, 0)), VMEM],
        out_specs=pl.BlockSpec((tokens, tile), lambda i: (0, i)),
        out_shape=pltpu.VMEM((tokens, units), BF16),
        compiler_params=SMALL,
        cost_estimate=FREE,
        name="turned",
    )(cotangent, pltpu.with_memory_space_constraint(earlier, pltpu.VMEM))


def assemble_kernel(local, kd, orders, at_ref, own_ref, *refs):
    out = refs[-1]
    out[:local] = own_ref[...]
    core = jnp.bitwise_and(at_ref[1], 1)
    at = local
    for i, order in enumerate(orders):
        mine, other = refs[2 * i], refs[2 * i + 1]
        bits = len(order) + 1
        blocks = mine.shape[bits - 1]
        for d in range(1 << bits):
            place = tuple((d >> bit) & 1 for bit in reversed(order))
            for b in range(blocks):
                rows = jnp.where(core == (d & 1), mine[place + (b,)], other[place + (b,)])
                out[at + b, d * kd : (d + 1) * kd, :] = rows
        at += blocks


def layer_kernel(nz, local, width, cols, chunk, at_ref, *refs):
    x_refs = refs[:nz]
    f_ref, cot_ref, s_ref = refs[nz : nz + 3]
    if chunk == 0:
        s_hbm, *dx_refs, og_ref, s_ref, mixed, back, arrived = refs[-(nz + 6) :]
        fetch = [pltpu.make_async_copy(s_hbm.at[j], s_ref.at[j], arrived.at[j]) for j in range(local)]
        for copy in fetch:
            copy.start()
    else:
        *dx_refs, og_ref, mixed, back = refs[-(nz + 3) :]
    z = at_ref[0]
    group = cols // local
    rows, out_width = dx_refs[0].shape[0], mixed.shape[2]
    here = slice(chunk * rows, (chunk + 1) * rows)
    low = lax.broadcasted_iota(jnp.int32, (rows, 2 * group), 1) < group

    for r in range(nz):
        for b in range(0, local, 2):
            one = dot(x_refs[r][:, b * width : (b + 1) * width], f_ref[r * local + b], ((1,), (0,)))
            two = dot(x_refs[r][:, (b + 1) * width : (b + 2) * width], f_ref[r * local + b + 1], ((1,), (0,)))
            at = (r * local + b) * group
            for h in range(local // 2):
                p = one[:, 2 * h * group : (2 * h + 2) * group]
                q = two[:, 2 * h * group : (2 * h + 2) * group]
                mixed[2 * h, :, at : at + 2 * group] = jnp.where(low, p, pltpu.roll(q, group, 1)).astype(BF16)
                mixed[2 * h + 1, :, at : at + 2 * group] = jnp.where(low, pltpu.roll(p, group, 1), q).astype(BF16)

    planes = [lax.rem(z + r, nz) for r in range(nz)]

    for j in range(local):
        if chunk == 0:
            fetch[j].wait()
        weight = jnp.concatenate(
            [s_ref[j, pl.ds(pl.multiple_of(p * cols, cols), cols), :] for p in planes], axis=0
        )
        pre_act = dot(mixed[j], weight, ((1,), (0,)))
        upstream = cot_ref[here, j * out_width : (j + 1) * out_width]
        pre_grad = (upstream.astype(F32) * gelu_slope(pre_act)).astype(BF16)
        back[j] = dot(pre_grad, weight, ((1,), (1,)))

    for r in range(nz):
        for b in range(0, local, 2):
            at = (r * local + b) * group
            one, two = [], []
            for h in range(local // 2):
                p = back[2 * h, :, at : at + 2 * group]
                q = back[2 * h + 1, :, at : at + 2 * group]
                one.append(jnp.where(low, p, pltpu.roll(q, group, 1)).astype(BF16))
                two.append(jnp.where(low, pltpu.roll(p, group, 1), q).astype(BF16))
            for i, part in ((b, one), (b + 1, two)):
                og = jnp.concatenate(part, axis=1)
                og_ref[r, :, i * cols : (i + 1) * cols] = og
                dx_refs[r][:, i * width : (i + 1) * width] = dot(
                    og, f_ref[r * local + i], ((1,), (1,))
                ).astype(dx_refs[r].dtype)


def layer(at, xs, first, second, cot, later, chunk, rows, nz, local, width, cols):
    out_width = second.shape[2]
    piece = (rows, local * width)
    return on_chip(
        functools.partial(layer_kernel, nz, local, width, cols, chunk),
        "layer",
        at,
        list(xs) + [first, cot] + (list(later) if chunk == 0 else [second]),
        [(piece, F32)]
        + [(piece, BF16)] * (nz - 1)
        + [((nz, rows, local * cols), BF16)]
        + [(second.shape, BF16)] * (chunk == 0),
        scratch_shapes=[
            pltpu.VMEM((local, rows, out_width), BF16),
            pltpu.VMEM((local, rows, out_width), F32),
        ]
        + [pltpu.SemaphoreType.DMA((local,))] * (chunk == 0),
        stored=[second] if chunk == 0 else (),
    )


def grad_kernel(nz, parts, local, width, cols, nd, at_ref, *refs):
    x_refs, og_refs = refs[: parts * nz], refs[parts * nz : parts * (nz + 1)]
    give, keep = refs[-2:]
    me = at_ref[1]
    kd = width // nd
    for r in range(nz):
        for b in range(local):
            x = jnp.concatenate(
                [x_refs[c * nz + r][:, b * width : (b + 1) * width] for c in range(parts)], axis=0
            )
            og = jnp.concatenate([og_refs[c][r, :, b * cols : (b + 1) * cols] for c in range(parts)], axis=0)
            term = dot(x, og, ((0,), (0,))).astype(BF16)
            for d in range(0, nd, 2):
                to = lax.div(jnp.bitwise_xor(me, d), 2)
                low, high = term[d * kd : (d + 1) * kd], term[(d + 1) * kd : (d + 2) * kd]
                odd = jnp.bitwise_and(me, 1) == 1
                keep[to, r * local + b] = jnp.where(odd, high, low)
                give[to, r * local + b] = jnp.where(odd, low, high)


def first_grad_terms(at, xs, ogs, later, nz, local, width, cols, nd):
    shape = (nd // 2, nz * local, width // nd, cols)
    return on_chip(
        functools.partial(grad_kernel, nz, len(ogs), local, width, cols, nd),
        "first_grad_terms",
        at,
        [a for x in xs for a in x] + list(ogs) + list(later),
        [(shape, BF16)] * 2,
    )


def sums_kernel(plan, at_ref, *refs):
    used = 0
    for i, has_got in enumerate(plan):
        total = refs[used][...]
        if has_got:
            total = (total.astype(F32) + refs[used + 1][...].astype(F32)).astype(BF16)
        used += 1 + has_got
        refs[i - len(plan)][...] = total


def sums(at, pairs, *earlier):
    return on_chip(
        functools.partial(sums_kernel, [got is not None for _, got in pairs]),
        "sums",
        at,
        [a for pair in pairs for a in pair if a is not None] + list(earlier),
        [(part.shape, BF16) for part, _ in pairs],
    )


def after(at, values, *earlier, stored=()):
    return on_chip(
        functools.partial(sums_kernel, [False] * len(values)),
        "after",
        at,
        list(values) + list(earlier),
        [(v.shape, v.dtype) for v in values],
        stored=stored,
    )


def mark_kernel(at_ref, *refs):
    refs[-1][...] = jnp.zeros_like(refs[-1])


def mark(at, values):
    held = [pltpu.with_memory_space_constraint(a, pltpu.VMEM) for a in values]
    return pl.pallas_call(
        mark_kernel,
        in_specs=[SMEM] + [VMEM] * len(held),
        out_specs=VMEM,
        out_shape=pltpu.VMEM((8, 128), F32),
        compiler_params=SMALL,
        cost_estimate=pl.CostEstimate(flops=10**10, bytes_accessed=32 << 20, transcendentals=0),
        name="mark",
    )(at, *held)


def halved_kernel(count, at_ref, *refs):
    low, high = refs[-2:]
    half, size = low.shape[0], refs[0].shape[0]
    for i in range(count):
        for b in range(size):
            at = i * size + b
            (low if at < half else high)[at % half] = refs[i][b]


def halved(at, blocks, *earlier):
    size, kd, cols = blocks[0].shape
    shape = (len(blocks) * size // 2, kd, cols)
    return on_chip(
        functools.partial(halved_kernel, len(blocks)), "halved", at, list(blocks) + list(earlier), [(shape, BF16)] * 2
    )


def join_kernel(count, at_ref, *refs):
    out = refs[-1]
    rows = refs[0].shape[0]
    for c in range(count):
        out[c * rows : (c + 1) * rows] = (refs[2 * c][...] + refs[2 * c + 1][...].astype(F32)).astype(BF16)


def join(at, pairs):
    held = [pltpu.with_memory_space_constraint(a, pltpu.VMEM) for pair in pairs for a in pair]
    rows, width = held[0].shape
    return pl.pallas_call(
        functools.partial(join_kernel, len(pairs)),
        in_specs=[SMEM] + [VMEM] * len(held),
        out_specs=VMEM,
        out_shape=jax.ShapeDtypeStruct((rows * len(pairs), width), BF16),
        compiler_params=SMALL,
        cost_estimate=FREE,
        name="join",
    )(at, *held)


def place_kernel(nz, local, cols, factor, at_ref, *refs):
    out = refs[-1]
    for r in range(nz):
        at = pl.multiple_of(lax.rem(at_ref[0] + nz - r, nz) * cols, cols)
        for b in range(local):
            out[:, b, pl.ds(at, cols)] = refs[r][b].astype(F32) * factor


def place(at, pieces, factor):
    nz = len(pieces)
    local, kd, cols = pieces[0].shape
    held = [pltpu.with_memory_space_constraint(a, pltpu.VMEM) for a in [*pieces, mark(at, pieces[1:])]]
    return pl.pallas_call(
        functools.partial(place_kernel, nz, local, cols, factor),
        in_specs=[SMEM] + [VMEM] * (nz + 1),
        out_specs=VMEM,
        out_shape=jax.ShapeDtypeStruct((kd, local, nz * cols), F32),
        compiler_params=SMALL,
        cost_estimate=FREE,
        name="place",
    )(at, *held)


def swap(bit, nd):
    return [(i, i ^ (1 << bit)) for i in range(nd)]


def ring_step(value, step, nz):
    return lax.ppermute(value, "tensor", [(i, (i + step) % nz) for i in range(nz)])


def double_over_dp(part, bit, d, nd):
    got = lax.ppermute(part, "dp", swap(bit, nd))
    upper = (d >> bit) & 1 == 1
    return jnp.stack([jnp.where(upper, got, part), jnp.where(upper, part, got)])


def body(inputs, first_factor, second_factor, cotangent):
    nz, nd = lax.axis_size("tensor"), lax.axis_size("dp")
    z, d = lax.axis_index("tensor"), lax.axis_index("dp")
    at = jnp.stack([z, d]).astype(jnp.int32)
    tokens_here = inputs.shape[0]
    width, local, out_width = first_factor.shape
    cols = out_width // nz
    kd = width // nd
    steps = (1, -1)
    rows = tokens_here // len(steps)
    bits = nd.bit_length() - 1
    orders = [list(range(1, bits)), list(range(bits - 1, 0, -1))]

    turn = lambda c, n: (-n * steps[c]) % nz
    xs = [[inputs[c * rows : (c + 1) * rows]] + [None] * (nz - 1) for c in range(len(steps))]
    for c in range(len(steps)):
        xs[c][turn(c, 1)] = ring_step(xs[c][0], steps[c], nz)

    def pass_on(n, *earlier, also=(), stored=()):
        arrived = [xs[c][turn(c, n - 1)] for c in range(len(steps))]
        came = after(at, arrived + list(also), mark(at, arrived), *earlier, stored=stored)
        for c in range(len(steps)):
            xs[c][turn(c, n - 1)] = came[c]
            xs[c][turn(c, n)] = ring_step(came[c], steps[c], nz)
        return came[len(steps) :]

    second = second_factor.transpose(1, 0, 2)
    sends = cut(at, first_factor, nz, nd)
    got = [ring_step(sends[r - 1], -r, nz) for r in range(1, nz)]
    if nz > 2:
        pass_on(2, *got, stored=[second])
    others = halved(at, got, *[xs[c][turn(c, 1)] for c in range(len(steps))])
    for k in range(max(bits - 1, 1)):
        if bits > 1:
            others = [double_over_dp(o, order[k], d, nd) for o, order in zip(others, orders)]
        if k == 0:
            cot = turned(cotangent, others[0])
            own = own_columns(at, first_factor, others[1], nz)
            if nz > 3:
                others = pass_on(3, own, cot, also=others)
    for n in range(4, nz):
        pass_on(n)
    pieces = []
    for o in others:
        pieces += [o, lax.ppermute(o, "dp", swap(0, nd))]
    first = on_chip(
        functools.partial(assemble_kernel, local, kd, orders),
        "assemble",
        at,
        [own] + pieces,
        [((nz * local, width, cols), BF16)],
    )[0]

    parts, ogs = [], []
    for c in range(len(steps)):
        later = [mark(at, [x[turn(i, nz - 1)] for i, x in enumerate(xs)])] if c == 0 else []
        res = layer(at, xs[c], first, second, cot, later, c, rows, nz, local, width, cols)
        parts.append(res[:nz])
        ogs.append(res[nz])
        second = res[-1] if c == 0 else second
    ring = [ring_step(parts[0][turn(0, 1)], steps[0], nz), None]

    def ring_next(n, *earlier):
        pairs, whose = [], []
        if n < nz:
            pairs.append((parts[0][turn(0, n)], ring[0]))
            whose.append(0)
        pairs.append((parts[1][turn(1, n - 1)], ring[1]))
        whose.append(1)
        sent = sums(at, pairs, *earlier)
        for c, send in zip(whose, sent):
            ring[c] = ring_step(send, steps[c], nz)
        return sent

    sent = ring_next(2)
    give, keep = first_grad_terms(at, xs, ogs, sent, nz, local, width, cols, nd)
    got = lax.ppermute(give, "dp", swap(0, nd))
    keep = keep.reshape([2] * (bits - 1) + list(keep.shape[1:]))
    got = got.reshape(keep.shape)
    half = nz * local // 2
    totals = []
    for i in range(2):
        cut_half = lambda a: a[(slice(None),) * (bits - 1) + (slice(i * half, (i + 1) * half),)]
        totals.append(cut_half(keep).astype(F32) + cut_half(got).astype(F32))
    left = [list(range(bits - 1, 0, -1)) for _ in range(2)]
    for k in range(bits - 1):
        give = []
        for i in range(2):
            axis = left[i].index(orders[i][k])
            left[i].remove(orders[i][k])
            pick = lambda n: lax.index_in_dim(totals[i], n, axis, keepdims=False)
            give.append(pick(1).astype(BF16))
            totals[i] = pick(0)
        if k == 0 and nz > 2:
            ring_next(3, *give)
        for i in range(2):
            totals[i] = totals[i] + lax.ppermute(give[i], "dp", swap(orders[i][k], nd)).astype(F32)
    blocks = jnp.concatenate(totals, axis=0).reshape(nz, local, kd, cols)
    give = [blocks[r].astype(BF16) for r in range(1, nz)]
    pieces = [blocks[0]] + [ring_step(give[r - 1], r, nz) for r in range(1, nz)]
    for n in range(4, nz + 1):
        ring_next(n, *give, ring[0])
    first_sum = place(at, pieces, (tokens_here * nd) ** (-0.5))
    return join(at, [(parts[c][0], ring[c]) for c in range(len(steps))]), first_sum


def plain_body(inputs, first_factor, second_factor, cotangent):
    tokens_here = inputs.shape[0]
    in_width, local, out_width = first_factor.shape
    blocks = local * lax.axis_size("tensor")
    group = out_width // blocks
    block_grouped = inputs.reshape(tokens_here, local, in_width)
    split_first = first_factor.reshape(in_width, local, blocks, group)
    outgoing = jnp.einsum("tlk,kljg->jlgt", block_grouped, split_first, preferred_element_type=F32).astype(BF16)
    arrived = lax.all_to_all(outgoing, "tensor", split_axis=0, concat_axis=1, tiled=True)
    mixed = arrived.reshape(local, out_width, tokens_here)
    pre_act = jnp.einsum("lmt,mln->lnt", mixed, second_factor, preferred_element_type=F32)
    upstream = cotangent.reshape(local, out_width, tokens_here).astype(F32)
    pre_grad = (upstream * gelu_slope(pre_act)).astype(BF16)
    mixed_grad = jnp.einsum("lnt,mln->lmt", pre_grad, second_factor, preferred_element_type=F32).astype(BF16)
    returned = lax.all_to_all(
        mixed_grad.reshape(local, blocks, group, tokens_here), "tensor", split_axis=1, concat_axis=0, tiled=True
    )
    input_grad = jnp.einsum("jlgt,kljg->tlk", returned, split_first, preferred_element_type=F32)
    input_grad = input_grad.reshape(tokens_here, local * in_width).astype(BF16)
    factor = (tokens_here * lax.axis_size("dp")) ** (-0.5)
    first_term = jnp.einsum("tlk,jlgt->kljg", block_grouped, returned, preferred_element_type=F32)
    first_term = first_term.reshape(in_width, local, out_width)
    first_sum = lax.psum_scatter(first_term, "dp", scatter_dimension=0, tiled=True)
    return input_grad, first_sum * factor


def solution(mesh):
    nz, nd = mesh.shape["tensor"], mesh.shape["dp"]

    def run(inputs, first_factor, second_factor, cotangent):
        width, local, _ = first_factor.shape
        fits = local % 2 == 0 and width % (16 * nd) == 0 and nd & (nd - 1) == 0
        return (body if fits else plain_body)(inputs, first_factor, second_factor, cotangent)

    return jax.shard_map(
        run,
        mesh=mesh,
        in_specs=(
            P("dp", "tensor"),
            P(None, "tensor", None),
            P(None, "tensor", None),
            P("tensor", "dp"),
        ),
        out_specs=(P("dp", "tensor"), P("dp", "tensor", None)),
        check_vma=False,
    )
```

```python
import functools

import jax
import jax.numpy as jnp
from jax import lax
from jax.experimental import pallas as pl
from jax.experimental.pallas import tpu as pltpu
from jax.sharding import PartitionSpec as P

BF16 = jnp.bfloat16
F32 = jnp.float32


def dot(a, b, dims):
    return lax.dot_general(a, b, (dims, ((), ())), preferred_element_type=F32)


def gelu_slope(v):
    c = 0.7978845608028654
    v2 = v * v
    t = jnp.tanh(v * (c + (c * 0.044715) * v2))
    return 0.5 + 0.5 * t + (0.5 * v) * (1.0 - t * t) * (c + (3.0 * c * 0.044715) * v2)


VMEM = pl.BlockSpec(memory_space=pltpu.VMEM)
SMALL = pltpu.CompilerParams(vmem_limit_bytes=16 << 20)
FREE = pl.CostEstimate(flops=0, bytes_accessed=0, transcendentals=0)
SMEM = pl.BlockSpec(memory_space=pltpu.SMEM)


def on_chip(kernel, name, at, operands, shapes, stored=(), limit=16 << 20, **more):
    held = [pltpu.with_memory_space_constraint(a, pltpu.VMEM) for a in operands]
    held += [pltpu.with_memory_space_constraint(a, pltpu.HBM) for a in stored]
    out = [pltpu.VMEM(shape, dtype) for shape, dtype in shapes]
    return pl.pallas_call(
        kernel,
        in_specs=[SMEM] + [VMEM] * len(operands) + [pl.BlockSpec(memory_space=pltpu.HBM)] * len(stored),
        out_specs=[VMEM] * len(out),
        out_shape=out,
        compiler_params=pltpu.CompilerParams(vmem_limit_bytes=limit),
        cost_estimate=FREE,
        name=name,
        **more,
    )(at, *held)


def cut_kernel(nz, local, cols, kd, at_ref, f_ref, *outs):
    for r in range(1, nz):
        col = pl.multiple_of(lax.rem(at_ref[0] + nz - r, nz) * cols, cols)
        for b in range(local):
            outs[r - 1][b] = f_ref[:, b, pl.ds(col, cols)]


def cut(at, first_factor, nz, nd):
    width, local, out_width = first_factor.shape
    kd, cols = width // nd, out_width // nz
    return pl.pallas_call(
        functools.partial(cut_kernel, nz, local, cols, kd),
        grid_spec=pltpu.PrefetchScalarGridSpec(
            num_scalar_prefetch=1,
            grid=(1,),
            in_specs=[pl.BlockSpec((kd, local, out_width), lambda i, at_ref: (at_ref[1], 0, 0))],
            out_specs=[pl.BlockSpec((local, kd, cols), lambda i, at_ref: (0, 0, 0))] * (nz - 1),
        ),
        out_shape=[pltpu.VMEM((local, kd, cols), BF16)] * (nz - 1),
        compiler_params=SMALL,
        cost_estimate=FREE,
        name="cut",
    )(at, first_factor)


def own_kernel(local, at_ref, f_ref, later_ref, out):
    for b in range(local):
        out[b] = f_ref[:, b, :]


def own_columns(at, first_factor, earlier, nz):
    width, local, out_width = first_factor.shape
    cols = out_width // nz
    return pl.pallas_call(
        functools.partial(own_kernel, local),
        grid_spec=pltpu.PrefetchScalarGridSpec(
            num_scalar_prefetch=1,
            grid=(1,),
            in_specs=[pl.BlockSpec((width, local, cols), lambda i, at_ref: (0, 0, at_ref[0])), VMEM],
            out_specs=pl.BlockSpec((local, width, cols), lambda i, at_ref: (0, 0, 0)),
        ),
        out_shape=pltpu.VMEM((local, width, cols), BF16),
        compiler_params=SMALL,
        cost_estimate=FREE,
        name="own_columns",
    )(at, first_factor, pltpu.with_memory_space_constraint(earlier, pltpu.VMEM))


def turn_kernel(x_ref, later_ref, out):
    out[...] = x_ref[...].T


def turned(cotangent, earlier, tile=512):
    units, tokens = cotangent.shape
    return pl.pallas_call(
        turn_kernel,
        grid=(units // tile,),
        in_specs=[pl.BlockSpec((tile, tokens), lambda i: (i, 0)), VMEM],
        out_specs=pl.BlockSpec((tokens, tile), lambda i: (0, i)),
        out_shape=pltpu.VMEM((tokens, units), BF16),
        compiler_params=SMALL,
        cost_estimate=FREE,
        name="turned",
    )(cotangent, pltpu.with_memory_space_constraint(earlier, pltpu.VMEM))


def assemble_kernel(local, kd, orders, at_ref, own_ref, *refs):
    out = refs[-1]
    out[:local] = own_ref[...]
    core = jnp.bitwise_and(at_ref[1], 1)
    at = local
    for i, order in enumerate(orders):
        mine, other = refs[2 * i], refs[2 * i + 1]
        bits = len(order) + 1
        blocks = mine.shape[bits - 1]
        for d in range(1 << bits):
            place = tuple((d >> bit) & 1 for bit in reversed(order))
            for b in range(blocks):
                rows = jnp.where(core == (d & 1), mine[place + (b,)], other[place + (b,)])
                out[at + b, d * kd : (d + 1) * kd, :] = rows
        at += blocks


def layer_kernel(nz, local, width, cols, chunk, at_ref, *refs):
    x_refs = refs[:nz]
    f_ref, cot_ref, s_ref = refs[nz : nz + 3]
    if chunk == 0:
        s_hbm, *dx_refs, og_ref, s_ref, mixed, back, arrived = refs[-(nz + 6) :]
        fetch = [pltpu.make_async_copy(s_hbm.at[j], s_ref.at[j], arrived.at[j]) for j in range(local)]
        for copy in fetch:
            copy.start()
    else:
        *dx_refs, og_ref, mixed, back = refs[-(nz + 3) :]
    z = at_ref[0]
    group = cols // local
    rows, out_width = dx_refs[0].shape[0], mixed.shape[2]
    here = slice(chunk * rows, (chunk + 1) * rows)
    low = lax.broadcasted_iota(jnp.int32, (rows, 2 * group), 1) < group

    for r in range(nz):
        for b in range(0, local, 2):
            one = dot(x_refs[r][:, b * width : (b + 1) * width], f_ref[r * local + b], ((1,), (0,)))
            two = dot(x_refs[r][:, (b + 1) * width : (b + 2) * width], f_ref[r * local + b + 1], ((1,), (0,)))
            at = (r * local + b) * group
            for h in range(local // 2):
                p = one[:, 2 * h * group : (2 * h + 2) * group]
                q = two[:, 2 * h * group : (2 * h + 2) * group]
                mixed[2 * h, :, at : at + 2 * group] = jnp.where(low, p, pltpu.roll(q, group, 1)).astype(BF16)
                mixed[2 * h + 1, :, at : at + 2 * group] = jnp.where(low, pltpu.roll(p, group, 1), q).astype(BF16)

    planes = [lax.rem(z + r, nz) for r in range(nz)]

    for j in range(local):
        if chunk == 0:
            fetch[j].wait()
        weight = jnp.concatenate(
            [s_ref[j, pl.ds(pl.multiple_of(p * cols, cols), cols), :] for p in planes], axis=0
        )
        pre_act = dot(mixed[j], weight, ((1,), (0,)))
        upstream = cot_ref[here, j * out_width : (j + 1) * out_width]
        pre_grad = (upstream.astype(F32) * gelu_slope(pre_act)).astype(BF16)
        back[j] = dot(pre_grad, weight, ((1,), (1,)))

    for r in range(nz):
        for b in range(0, local, 2):
            at = (r * local + b) * group
            one, two = [], []
            for h in range(local // 2):
                p = back[2 * h, :, at : at + 2 * group]
                q = back[2 * h + 1, :, at : at + 2 * group]
                one.append(jnp.where(low, p, pltpu.roll(q, group, 1)).astype(BF16))
                two.append(jnp.where(low, pltpu.roll(p, group, 1), q).astype(BF16))
            for i, part in ((b, one), (b + 1, two)):
                og = jnp.concatenate(part, axis=1)
                og_ref[r, :, i * cols : (i + 1) * cols] = og
                dx_refs[r][:, i * width : (i + 1) * width] = dot(
                    og, f_ref[r * local + i], ((1,), (1,))
                ).astype(dx_refs[r].dtype)


def layer(at, xs, first, second, cot, later, chunk, rows, nz, local, width, cols):
    out_width = second.shape[2]
    piece = (rows, local * width)
    return on_chip(
        functools.partial(layer_kernel, nz, local, width, cols, chunk),
        "layer",
        at,
        list(xs) + [first, cot] + (list(later) if chunk == 0 else [second]),
        [(piece, F32)]
        + [(piece, BF16)] * (nz - 1)
        + [((nz, rows, local * cols), BF16)]
        + [(second.shape, BF16)] * (chunk == 0),
        scratch_shapes=[
            pltpu.VMEM((local, rows, out_width), BF16),
            pltpu.VMEM((local, rows, out_width), F32),
        ]
        + [pltpu.SemaphoreType.DMA((local,))] * (chunk == 0),
        stored=[second] if chunk == 0 else (),
    )


def grad_kernel(nz, parts, local, width, cols, nd, at_ref, *refs):
    x_refs, og_refs = refs[: parts * nz], refs[parts * nz : parts * (nz + 1)]
    give, keep = refs[-2:]
    me = at_ref[1]
    kd = width // nd
    for r in range(nz):
        for b in range(local):
            x = jnp.concatenate(
                [x_refs[c * nz + r][:, b * width : (b + 1) * width] for c in range(parts)], axis=0
            )
            og = jnp.concatenate([og_refs[c][r, :, b * cols : (b + 1) * cols] for c in range(parts)], axis=0)
            term = dot(x, og, ((0,), (0,))).astype(BF16)
            for d in range(0, nd, 2):
                to = lax.div(jnp.bitwise_xor(me, d), 2)
                low, high = term[d * kd : (d + 1) * kd], term[(d + 1) * kd : (d + 2) * kd]
                odd = jnp.bitwise_and(me, 1) == 1
                keep[to, r * local + b] = jnp.where(odd, high, low)
                give[to, r * local + b] = jnp.where(odd, low, high)


def first_grad_terms(at, xs, ogs, later, nz, local, width, cols, nd):
    shape = (nd // 2, nz * local, width // nd, cols)
    return on_chip(
        functools.partial(grad_kernel, nz, len(ogs), local, width, cols, nd),
        "first_grad_terms",
        at,
        [a for x in xs for a in x] + list(ogs) + list(later),
        [(shape, BF16)] * 2,
    )


def sums_kernel(plan, at_ref, *refs):
    used = 0
    for i, has_got in enumerate(plan):
        total = refs[used][...]
        if has_got:
            total = (total.astype(F32) + refs[used + 1][...].astype(F32)).astype(BF16)
        used += 1 + has_got
        refs[i - len(plan)][...] = total


def sums(at, pairs, *earlier):
    return on_chip(
        functools.partial(sums_kernel, [got is not None for _, got in pairs]),
        "sums",
        at,
        [a for pair in pairs for a in pair if a is not None] + list(earlier),
        [(part.shape, BF16) for part, _ in pairs],
    )


def after(at, values, *earlier, stored=()):
    return on_chip(
        functools.partial(sums_kernel, [False] * len(values)),
        "after",
        at,
        list(values) + list(earlier),
        [(v.shape, v.dtype) for v in values],
        stored=stored,
    )


def mark_kernel(at_ref, *refs):
    refs[-1][...] = jnp.zeros_like(refs[-1])


def mark(at, values):
    held = [pltpu.with_memory_space_constraint(a, pltpu.VMEM) for a in values]
    return pl.pallas_call(
        mark_kernel,
        in_specs=[SMEM] + [VMEM] * len(held),
        out_specs=VMEM,
        out_shape=pltpu.VMEM((8, 128), F32),
        compiler_params=SMALL,
        cost_estimate=pl.CostEstimate(flops=10**10, bytes_accessed=32 << 20, transcendentals=0),
        name="mark",
    )(at, *held)


def halved_kernel(count, at_ref, *refs):
    low, high = refs[-2:]
    half, size = low.shape[0], refs[0].shape[0]
    for i in range(count):
        for b in range(size):
            at = i * size + b
            (low if at < half else high)[at % half] = refs[i][b]


def halved(at, blocks, *earlier):
    size, kd, cols = blocks[0].shape
    shape = (len(blocks) * size // 2, kd, cols)
    return on_chip(
        functools.partial(halved_kernel, len(blocks)), "halved", at, list(blocks) + list(earlier), [(shape, BF16)] * 2
    )


def join_kernel(at_ref, *refs):
    out = refs[-1]
    rows = refs[0].shape[0]
    for c in range(2):
        own, up, down = [ref[...].astype(F32) for ref in refs[3 * c : 3 * c + 3]]
        out[c * rows : (c + 1) * rows] = (own + up + down).astype(BF16)


def join(at, halves):
    held = [pltpu.with_memory_space_constraint(a, pltpu.VMEM) for half in halves for a in half]
    rows, width = held[0].shape
    return pl.pallas_call(
        join_kernel,
        in_specs=[SMEM] + [VMEM] * len(held),
        out_specs=VMEM,
        out_shape=jax.ShapeDtypeStruct((rows * 2, width), BF16),
        compiler_params=SMALL,
        cost_estimate=FREE,
        name="join",
    )(at, *held)


def place_kernel(nz, local, cols, factor, at_ref, *refs):
    out = refs[-1]
    for r in range(nz):
        at = pl.multiple_of(lax.rem(at_ref[0] + nz - r, nz) * cols, cols)
        for b in range(local):
            out[:, b, pl.ds(at, cols)] = refs[r][b].astype(F32) * factor


def place(at, pieces, factor):
    nz = len(pieces)
    local, kd, cols = pieces[0].shape
    held = [pltpu.with_memory_space_constraint(a, pltpu.VMEM) for a in [*pieces, mark(at, pieces[1:])]]
    return pl.pallas_call(
        functools.partial(place_kernel, nz, local, cols, factor),
        in_specs=[SMEM] + [VMEM] * (nz + 1),
        out_specs=VMEM,
        out_shape=jax.ShapeDtypeStruct((kd, local, nz * cols), F32),
        compiler_params=SMALL,
        cost_estimate=FREE,
        name="place",
    )(at, *held)


def swap(bit, nd):
    return [(i, i ^ (1 << bit)) for i in range(nd)]


def ring_step(value, step, nz):
    return lax.ppermute(value, "tensor", [(i, (i + step) % nz) for i in range(nz)])


def double_over_dp(part, bit, d, nd):
    got = lax.ppermute(part, "dp", swap(bit, nd))
    upper = (d >> bit) & 1 == 1
    return jnp.stack([jnp.where(upper, got, part), jnp.where(upper, part, got)])


def body(inputs, first_factor, second_factor, cotangent):
    nz, nd = lax.axis_size("tensor"), lax.axis_size("dp")
    z, d = lax.axis_index("tensor"), lax.axis_index("dp")
    at = jnp.stack([z, d]).astype(jnp.int32)
    tokens_here = inputs.shape[0]
    width, local, out_width = first_factor.shape
    cols = out_width // nz
    kd = width // nd
    rows = tokens_here // 2
    bits = nd.bit_length() - 1
    orders = [list(range(1, bits)), list(range(bits - 1, 0, -1))]

    xs = [[inputs[c * rows : (c + 1) * rows]] + [None] * (nz - 1) for c in range(2)]
    xs[0][3] = ring_step(xs[0][0], 1, nz)
    xs[0][1] = ring_step(xs[0][0], -1, nz)
    second = second_factor.transpose(1, 0, 2)
    sends = cut(at, first_factor, nz, nd)
    got = [ring_step(sends[r - 1], -r, nz) for r in range(1, nz)]
    near = mark(at, [xs[0][3], xs[0][1]])
    xs[0][3], xs[1][0] = after(at, [xs[0][3], xs[1][0]], near, *got, stored=[second])
    xs[0][2] = ring_step(xs[0][3], 1, nz)
    xs[1][1] = ring_step(xs[1][0], -1, nz)
    xs[1][3] = ring_step(xs[1][0], 1, nz)

    others = halved(at, got, xs[0][3])
    for k in range(max(bits - 1, 1)):
        if bits > 1:
            others = [double_over_dp(o, order[k], d, nd) for o, order in zip(others, orders)]
        if k == 0:
            cot = turned(cotangent, others[0])
            own = own_columns(at, first_factor, others[1], nz)
    pieces = []
    for o in others:
        pieces += [o, lax.ppermute(o, "dp", swap(0, nd))]
    first = on_chip(
        functools.partial(assemble_kernel, local, kd, orders),
        "assemble",
        at,
        [own] + pieces,
        [((nz * local, width, cols), BF16)],
    )[0]
    far = mark(at, [xs[0][2], xs[1][1], xs[1][3]])
    (xs[1][1],) = after(at, [xs[1][1]], far)
    xs[1][2] = ring_step(xs[1][1], -1, nz)

    low = layer(at, xs[0], first, second, cot, [xs[1][1]], 0, rows, nz, local, width, cols)
    low_far = ring_step(low[2], 1, nz)
    low_down = ring_step(low[3], -1, nz)
    high = layer(at, xs[1], first, low[-1], cot, [], 1, rows, nz, local, width, cols)
    high_far = ring_step(high[2], -1, nz)
    high_up = ring_step(high[1], 1, nz)
    sent = sums(at, [(low[1], low_far)], mark(at, [low_far, low_down]))
    low_up = ring_step(sent[0], 1, nz)

    give, keep = first_grad_terms(at, xs, [low[nz], high[nz]], sent, nz, local, width, cols, nd)
    got = lax.ppermute(give, "dp", swap(0, nd))
    keep = keep.reshape([2] * (bits - 1) + list(keep.shape[1:]))
    got = got.reshape(keep.shape)
    half = nz * local // 2
    totals = []
    for i in range(2):
        cut_half = lambda a: a[(slice(None),) * (bits - 1) + (slice(i * half, (i + 1) * half),)]
        totals.append(cut_half(keep).astype(F32) + cut_half(got).astype(F32))
    left = [list(range(bits - 1, 0, -1)) for _ in range(2)]
    for k in range(bits - 1):
        give = []
        for i in range(2):
            axis = left[i].index(orders[i][k])
            left[i].remove(orders[i][k])
            pick = lambda n: lax.index_in_dim(totals[i], n, axis, keepdims=False)
            give.append(pick(1).astype(BF16))
            totals[i] = pick(0)
        for i in range(2):
            totals[i] = totals[i] + lax.ppermute(give[i], "dp", swap(orders[i][k], nd)).astype(F32)
    sent = sums(at, [(high[3], high_far)], mark(at, [high_far, high_up, low_up]), *give)
    high_down = ring_step(sent[0], -1, nz)
    blocks = jnp.concatenate(totals, axis=0).reshape(nz, local, kd, cols)
    give = [blocks[r].astype(BF16) for r in range(1, nz)]
    pieces = [blocks[0]] + [ring_step(give[r - 1], r, nz) for r in range(1, nz)]
    first_sum = place(at, pieces, (tokens_here * nd) ** (-0.5))
    return join(at, [(low[0], low_up, low_down), (high[0], high_up, high_down)]), first_sum


def plain_body(inputs, first_factor, second_factor, cotangent):
    tokens_here = inputs.shape[0]
    in_width, local, out_width = first_factor.shape
    blocks = local * lax.axis_size("tensor")
    group = out_width // blocks
    block_grouped = inputs.reshape(tokens_here, local, in_width)
    split_first = first_factor.reshape(in_width, local, blocks, group)
    outgoing = jnp.einsum("tlk,kljg->jlgt", block_grouped, split_first, preferred_element_type=F32).astype(BF16)
    arrived = lax.all_to_all(outgoing, "tensor", split_axis=0, concat_axis=1, tiled=True)
    mixed = arrived.reshape(local, out_width, tokens_here)
    pre_act = jnp.einsum("lmt,mln->lnt", mixed, second_factor, preferred_element_type=F32)
    upstream = cotangent.reshape(local, out_width, tokens_here).astype(F32)
    pre_grad = (upstream * gelu_slope(pre_act)).astype(BF16)
    mixed_grad = jnp.einsum("lnt,mln->lmt", pre_grad, second_factor, preferred_element_type=F32).astype(BF16)
    returned = lax.all_to_all(
        mixed_grad.reshape(local, blocks, group, tokens_here), "tensor", split_axis=1, concat_axis=0, tiled=True
    )
    input_grad = jnp.einsum("jlgt,kljg->tlk", returned, split_first, preferred_element_type=F32)
    input_grad = input_grad.reshape(tokens_here, local * in_width).astype(BF16)
    factor = (tokens_here * lax.axis_size("dp")) ** (-0.5)
    first_term = jnp.einsum("tlk,jlgt->kljg", block_grouped, returned, preferred_element_type=F32)
    first_term = first_term.reshape(in_width, local, out_width)
    first_sum = lax.psum_scatter(first_term, "dp", scatter_dimension=0, tiled=True)
    return input_grad, first_sum * factor


def solution(mesh):
    nz, nd = mesh.shape["tensor"], mesh.shape["dp"]

    def run(inputs, first_factor, second_factor, cotangent):
        width, local, _ = first_factor.shape
        fits = nz == 4 and local % 2 == 0 and width % (16 * nd) == 0 and nd & (nd - 1) == 0
        return (body if fits else plain_body)(inputs, first_factor, second_factor, cotangent)

    return jax.shard_map(
        run,
        mesh=mesh,
        in_specs=(
            P("dp", "tensor"),
            P(None, "tensor", None),
            P(None, "tensor", None),
            P("tensor", "dp"),
        ),
        out_specs=(P("dp", "tensor"), P("dp", "tensor", None)),
        check_vma=False,
    )
```

```python
import functools

import jax
import jax.numpy as jnp
from jax import lax
from jax.experimental import pallas as pl
from jax.experimental.pallas import tpu as pltpu
from jax.sharding import PartitionSpec as P

BF16 = jnp.bfloat16
F32 = jnp.float32


def dot(a, b, dims):
    return lax.dot_general(a, b, (dims, ((), ())), preferred_element_type=F32)


def gelu_slope(v):
    c = 0.7978845608028654
    v2 = v * v
    t = jnp.tanh(v * (c + (c * 0.044715) * v2))
    return 0.5 + 0.5 * t + (0.5 * v) * (1.0 - t * t) * (c + (3.0 * c * 0.044715) * v2)


VMEM = pl.BlockSpec(memory_space=pltpu.VMEM)
SMALL = pltpu.CompilerParams(vmem_limit_bytes=16 << 20)
FREE = pl.CostEstimate(flops=0, bytes_accessed=0, transcendentals=0)
SMEM = pl.BlockSpec(memory_space=pltpu.SMEM)


def on_chip(kernel, name, at, operands, shapes, stored=(), limit=16 << 20, **more):
    held = [pltpu.with_memory_space_constraint(a, pltpu.VMEM) for a in operands]
    held += [pltpu.with_memory_space_constraint(a, pltpu.HBM) for a in stored]
    out = [pltpu.VMEM(shape, dtype) for shape, dtype in shapes]
    return pl.pallas_call(
        kernel,
        in_specs=[SMEM] + [VMEM] * len(operands) + [pl.BlockSpec(memory_space=pltpu.HBM)] * len(stored),
        out_specs=[VMEM] * len(out),
        out_shape=out,
        compiler_params=pltpu.CompilerParams(vmem_limit_bytes=limit),
        cost_estimate=FREE,
        name=name,
        **more,
    )(at, *held)


def cut_kernel(nz, local, cols, kd, at_ref, f_ref, *outs):
    for r in range(1, nz):
        col = pl.multiple_of(lax.rem(at_ref[0] + nz - r, nz) * cols, cols)
        for b in range(local):
            outs[r - 1][b] = f_ref[:, b, pl.ds(col, cols)]


def cut(at, first_factor, nz, nd):
    width, local, out_width = first_factor.shape
    kd, cols = width // nd, out_width // nz
    return pl.pallas_call(
        functools.partial(cut_kernel, nz, local, cols, kd),
        grid_spec=pltpu.PrefetchScalarGridSpec(
            num_scalar_prefetch=1,
            grid=(1,),
            in_specs=[pl.BlockSpec((kd, local, out_width), lambda i, at_ref: (at_ref[1], 0, 0))],
            out_specs=[pl.BlockSpec((local, kd, cols), lambda i, at_ref: (0, 0, 0))] * (nz - 1),
        ),
        out_shape=[pltpu.VMEM((local, kd, cols), BF16)] * (nz - 1),
        compiler_params=SMALL,
        cost_estimate=FREE,
        name="cut",
    )(at, first_factor)


def own_kernel(local, at_ref, f_ref, later_ref, out):
    for b in range(local):
        out[b] = f_ref[:, b, :]


def own_columns(at, first_factor, earlier, nz):
    width, local, out_width = first_factor.shape
    cols = out_width // nz
    return pl.pallas_call(
        functools.partial(own_kernel, local),
        grid_spec=pltpu.PrefetchScalarGridSpec(
            num_scalar_prefetch=1,
            grid=(1,),
            in_specs=[pl.BlockSpec((width, local, cols), lambda i, at_ref: (0, 0, at_ref[0])), VMEM],
            out_specs=pl.BlockSpec((local, width, cols), lambda i, at_ref: (0, 0, 0)),
        ),
        out_shape=pltpu.VMEM((local, width, cols), BF16),
        compiler_params=SMALL,
        cost_estimate=FREE,
        name="own_columns",
    )(at, first_factor, pltpu.with_memory_space_constraint(earlier, pltpu.VMEM))


def turn_kernel(x_ref, later_ref, out):
    out[...] = x_ref[...].T


def turned(cotangent, earlier, tile=512):
    units, tokens = cotangent.shape
    return pl.pallas_call(
        turn_kernel,
        grid=(units // tile,),
        in_specs=[pl.BlockSpec((tile, tokens), lambda i: (i, 0)), VMEM],
        out_specs=pl.BlockSpec((tokens, tile), lambda i: (0, i)),
        out_shape=pltpu.VMEM((tokens, units), BF16),
        compiler_params=SMALL,
        cost_estimate=FREE,
        name="turned",
    )(cotangent, pltpu.with_memory_space_constraint(earlier, pltpu.VMEM))


def assemble_kernel(local, kd, orders, at_ref, own_ref, *refs):
    out = refs[-1]
    out[:local] = own_ref[...]
    core = jnp.bitwise_and(at_ref[1], 1)
    at = local
    for i, order in enumerate(orders):
        mine, other = refs[2 * i], refs[2 * i + 1]
        bits = len(order) + 1
        blocks = mine.shape[bits - 1]
        for d in range(1 << bits):
            place = tuple((d >> bit) & 1 for bit in reversed(order))
            for b in range(blocks):
                rows = jnp.where(core == (d & 1), mine[place + (b,)], other[place + (b,)])
                out[at + b, d * kd : (d + 1) * kd, :] = rows
        at += blocks


def layer_kernel(nz, local, width, cols, chunk, at_ref, *refs):
    x_refs = refs[:nz]
    f_ref, cot_ref, s_ref = refs[nz : nz + 3]
    if chunk == 0:
        s_hbm, *dx_refs, og_ref, s_ref, mixed, back, arrived = refs[-(nz + 6) :]
        fetch = [pltpu.make_async_copy(s_hbm.at[j], s_ref.at[j], arrived.at[j]) for j in range(local)]
        for copy in fetch:
            copy.start()
    else:
        *dx_refs, og_ref, mixed, back = refs[-(nz + 3) :]
    z = at_ref[0]
    group = cols // local
    rows, out_width = dx_refs[0].shape[0], mixed.shape[2]
    here = slice(chunk * rows, (chunk + 1) * rows)
    low = lax.broadcasted_iota(jnp.int32, (rows, 2 * group), 1) < group

    for r in range(nz):
        for b in range(0, local, 2):
            one = dot(x_refs[r][:, b * width : (b + 1) * width], f_ref[r * local + b], ((1,), (0,)))
            two = dot(x_refs[r][:, (b + 1) * width : (b + 2) * width], f_ref[r * local + b + 1], ((1,), (0,)))
            at = (r * local + b) * group
            for h in range(local // 2):
                p = one[:, 2 * h * group : (2 * h + 2) * group]
                q = two[:, 2 * h * group : (2 * h + 2) * group]
                mixed[2 * h, :, at : at + 2 * group] = jnp.where(low, p, pltpu.roll(q, group, 1)).astype(BF16)
                mixed[2 * h + 1, :, at : at + 2 * group] = jnp.where(low, pltpu.roll(p, group, 1), q).astype(BF16)

    planes = [lax.rem(z + r, nz) for r in range(nz)]

    for j in range(local):
        if chunk == 0:
            fetch[j].wait()
        weight = jnp.concatenate(
            [s_ref[j, pl.ds(pl.multiple_of(p * cols, cols), cols), :] for p in planes], axis=0
        )
        pre_act = dot(mixed[j], weight, ((1,), (0,)))
        upstream = cot_ref[here, j * out_width : (j + 1) * out_width]
        pre_grad = (upstream.astype(F32) * gelu_slope(pre_act)).astype(BF16)
        back[j] = dot(pre_grad, weight, ((1,), (1,)))

    for r in range(nz):
        for b in range(0, local, 2):
            at = (r * local + b) * group
            one, two = [], []
            for h in range(local // 2):
                p = back[2 * h, :, at : at + 2 * group]
                q = back[2 * h + 1, :, at : at + 2 * group]
                one.append(jnp.where(low, p, pltpu.roll(q, group, 1)).astype(BF16))
                two.append(jnp.where(low, pltpu.roll(p, group, 1), q).astype(BF16))
            for i, part in ((b, one), (b + 1, two)):
                og = jnp.concatenate(part, axis=1)
                og_ref[r, :, i * cols : (i + 1) * cols] = og
                dx_refs[r][:, i * width : (i + 1) * width] = dot(
                    og, f_ref[r * local + i], ((1,), (1,))
                ).astype(dx_refs[r].dtype)


def layer(at, xs, first, second, cot, later, chunk, rows, nz, local, width, cols):
    out_width = second.shape[2]
    piece = (rows, local * width)
    return on_chip(
        functools.partial(layer_kernel, nz, local, width, cols, chunk),
        "layer",
        at,
        list(xs) + [first, cot] + (list(later) if chunk == 0 else [second]),
        [(piece, F32)]
        + [(piece, BF16)] * (nz - 1)
        + [((nz, rows, local * cols), BF16)]
        + [(second.shape, BF16)] * (chunk == 0),
        scratch_shapes=[
            pltpu.VMEM((local, rows, out_width), BF16),
            pltpu.VMEM((local, rows, out_width), F32),
        ]
        + [pltpu.SemaphoreType.DMA((local,))] * (chunk == 0),
        stored=[second] if chunk == 0 else (),
    )


def grad_kernel(nz, parts, local, width, cols, nd, at_ref, *refs):
    x_refs, og_refs = refs[: parts * nz], refs[parts * nz : parts * (nz + 1)]
    give, keep = refs[-2:]
    me = at_ref[1]
    kd = width // nd
    for r in range(nz):
        for b in range(local):
            x = jnp.concatenate(
                [x_refs[c * nz + r][:, b * width : (b + 1) * width] for c in range(parts)], axis=0
            )
            og = jnp.concatenate([og_refs[c][r, :, b * cols : (b + 1) * cols] for c in range(parts)], axis=0)
            term = dot(x, og, ((0,), (0,))).astype(BF16)
            for d in range(0, nd, 2):
                to = lax.div(jnp.bitwise_xor(me, d), 2)
                low, high = term[d * kd : (d + 1) * kd], term[(d + 1) * kd : (d + 2) * kd]
                odd = jnp.bitwise_and(me, 1) == 1
                keep[to, r * local + b] = jnp.where(odd, high, low)
                give[to, r * local + b] = jnp.where(odd, low, high)


def first_grad_terms(at, xs, ogs, later, nz, local, width, cols, nd):
    shape = (nd // 2, nz * local, width // nd, cols)
    return on_chip(
        functools.partial(grad_kernel, nz, len(ogs), local, width, cols, nd),
        "first_grad_terms",
        at,
        [a for x in xs for a in x] + list(ogs) + list(later),
        [(shape, BF16)] * 2,
    )


def sums_kernel(plan, at_ref, *refs):
    used = 0
    for i, has_got in enumerate(plan):
        total = refs[used][...]
        if has_got:
            total = (total.astype(F32) + refs[used + 1][...].astype(F32)).astype(BF16)
        used += 1 + has_got
        refs[i - len(plan)][...] = total


def sums(at, pairs, *earlier):
    return on_chip(
        functools.partial(sums_kernel, [got is not None for _, got in pairs]),
        "sums",
        at,
        [a for pair in pairs for a in pair if a is not None] + list(earlier),
        [(part.shape, BF16) for part, _ in pairs],
    )


def after(at, values, *earlier, stored=()):
    return on_chip(
        functools.partial(sums_kernel, [False] * len(values)),
        "after",
        at,
        list(values) + list(earlier),
        [(v.shape, v.dtype) for v in values],
        stored=stored,
    )


def mark_kernel(at_ref, *refs):
    refs[-1][...] = jnp.zeros_like(refs[-1])


def mark(at, values):
    held = [pltpu.with_memory_space_constraint(a, pltpu.VMEM) for a in values]
    return pl.pallas_call(
        mark_kernel,
        in_specs=[SMEM] + [VMEM] * len(held),
        out_specs=VMEM,
        out_shape=pltpu.VMEM((8, 128), F32),
        compiler_params=SMALL,
        cost_estimate=pl.CostEstimate(flops=10**10, bytes_accessed=32 << 20, transcendentals=0),
        name="mark",
    )(at, *held)


def halved_kernel(count, at_ref, *refs):
    low, high = refs[-2:]
    half, size = low.shape[0], refs[0].shape[0]
    for i in range(count):
        for b in range(size):
            at = i * size + b
            (low if at < half else high)[at % half] = refs[i][b]


def halved(at, blocks, *earlier):
    size, kd, cols = blocks[0].shape
    shape = (len(blocks) * size // 2, kd, cols)
    return on_chip(
        functools.partial(halved_kernel, len(blocks)), "halved", at, list(blocks) + list(earlier), [(shape, BF16)] * 2
    )


def join_kernel(at_ref, *refs):
    out = refs[-1]
    rows = refs[0].shape[0]
    for c in range(2):
        own, up, down = [ref[...].astype(F32) for ref in refs[3 * c : 3 * c + 3]]
        out[c * rows : (c + 1) * rows] = (own + up + down).astype(BF16)


def join(at, halves):
    late = mark(at, [halves[0][1], halves[1][1]])
    held = [pltpu.with_memory_space_constraint(a, pltpu.VMEM) for half in halves for a in half] + [late]
    rows, width = held[0].shape
    return pl.pallas_call(
        join_kernel,
        in_specs=[SMEM] + [VMEM] * len(held),
        out_specs=VMEM,
        out_shape=jax.ShapeDtypeStruct((rows * 2, width), BF16),
        compiler_params=SMALL,
        cost_estimate=FREE,
        name="join",
    )(at, *held)


def place_kernel(nz, local, cols, factor, at_ref, *refs):
    out = refs[-1]
    for r in range(nz):
        at = pl.multiple_of(lax.rem(at_ref[0] + nz - r, nz) * cols, cols)
        for b in range(local):
            out[:, b, pl.ds(at, cols)] = refs[r][b].astype(F32) * factor


def place(at, pieces, factor):
    nz = len(pieces)
    local, kd, cols = pieces[0].shape
    held = [pltpu.with_memory_space_constraint(a, pltpu.VMEM) for a in [*pieces, mark(at, pieces[1:])]]
    return pl.pallas_call(
        functools.partial(place_kernel, nz, local, cols, factor),
        in_specs=[SMEM] + [VMEM] * (nz + 1),
        out_specs=VMEM,
        out_shape=jax.ShapeDtypeStruct((kd, local, nz * cols), F32),
        compiler_params=SMALL,
        cost_estimate=FREE,
        name="place",
    )(at, *held)


def swap(bit, nd):
    return [(i, i ^ (1 << bit)) for i in range(nd)]


def ring_step(value, step, nz):
    return lax.ppermute(value, "tensor", [(i, (i + step) % nz) for i in range(nz)])


def double_over_dp(part, bit, d, nd):
    got = lax.ppermute(part, "dp", swap(bit, nd))
    upper = (d >> bit) & 1 == 1
    return jnp.stack([jnp.where(upper, got, part), jnp.where(upper, part, got)])


def body(inputs, first_factor, second_factor, cotangent):
    nz, nd = lax.axis_size("tensor"), lax.axis_size("dp")
    z, d = lax.axis_index("tensor"), lax.axis_index("dp")
    at = jnp.stack([z, d]).astype(jnp.int32)
    tokens_here = inputs.shape[0]
    width, local, out_width = first_factor.shape
    cols = out_width // nz
    kd = width // nd
    rows = tokens_here // 2
    bits = nd.bit_length() - 1
    orders = [list(range(1, bits)), list(range(bits - 1, 0, -1))]

    xs = [[inputs[c * rows : (c + 1) * rows]] + [None] * (nz - 1) for c in range(2)]
    xs[0][3] = ring_step(xs[0][0], 1, nz)
    xs[0][1] = ring_step(xs[0][0], -1, nz)
    second = second_factor.transpose(1, 0, 2)
    sends = cut(at, first_factor, nz, nd)
    got = [ring_step(sends[r - 1], -r, nz) for r in range(1, nz)]
    near = mark(at, [xs[0][3], xs[0][1]])
    xs[0][3], xs[1][0] = after(at, [xs[0][3], xs[1][0]], near, *got, stored=[second])
    xs[0][2] = ring_step(xs[0][3], 1, nz)
    xs[1][1] = ring_step(xs[1][0], -1, nz)
    xs[1][3] = ring_step(xs[1][0], 1, nz)

    others = halved(at, got, xs[0][3])
    for k in range(bits - 1):
        others = [double_over_dp(o, order[k], d, nd) for o, order in zip(others, orders)]
        if k == 0:
            own = own_columns(at, first_factor, others[0], nz)
    cot = turned(cotangent, others[1])
    pieces = []
    for o in others:
        pieces += [o, lax.ppermute(o, "dp", swap(0, nd))]
    first = on_chip(
        functools.partial(assemble_kernel, local, kd, orders),
        "assemble",
        at,
        [own] + pieces,
        [((nz * local, width, cols), BF16)],
    )[0]
    far = mark(at, [xs[0][2], xs[1][1], xs[1][3], own, cot])
    (xs[1][1],) = after(at, [xs[1][1]], far)
    xs[1][2] = ring_step(xs[1][1], -1, nz)

    low = layer(at, xs[0], first, second, cot, [xs[1][1]], 0, rows, nz, local, width, cols)
    low_far = ring_step(low[2], 1, nz)
    low_down = ring_step(low[3], -1, nz)
    high = layer(at, xs[1], first, low[-1], cot, [], 1, rows, nz, local, width, cols)
    high_far = ring_step(high[2], -1, nz)
    high_up = ring_step(high[1], 1, nz)
    give, keep = first_grad_terms(at, xs, [low[nz], high[nz]], [], nz, local, width, cols, nd)
    sent = sums(at, [(low[1], low_far)], mark(at, [low_far, low_down, give]))
    low_up = ring_step(sent[0], 1, nz)

    got = lax.ppermute(give, "dp", swap(0, nd))
    keep = keep.reshape([2] * (bits - 1) + list(keep.shape[1:]))
    got = got.reshape(keep.shape)
    half = nz * local // 2
    totals = []
    for i in range(2):
        cut_half = lambda a: a[(slice(None),) * (bits - 1) + (slice(i * half, (i + 1) * half),)]
        totals.append(cut_half(keep).astype(F32) + cut_half(got).astype(F32))
    left = [list(range(bits - 1, 0, -1)) for _ in range(2)]
    for k in range(bits - 1):
        give = []
        for i in range(2):
            axis = left[i].index(orders[i][k])
            left[i].remove(orders[i][k])
            pick = lambda n: lax.index_in_dim(totals[i], n, axis, keepdims=False)
            give.append(pick(1).astype(BF16))
            totals[i] = pick(0)
        if k == 0:
            sent = sums(at, [(high[3], high_far)], mark(at, [high_far, *give]))
        for i in range(2):
            totals[i] = totals[i] + lax.ppermute(give[i], "dp", swap(orders[i][k], nd)).astype(F32)
    high_down = ring_step(sent[0], -1, nz)
    blocks = jnp.concatenate(totals, axis=0).reshape(nz, local, kd, cols)
    give = [blocks[r].astype(BF16) for r in range(1, nz)]
    pieces = [blocks[0]] + [ring_step(give[r - 1], r, nz) for r in range(1, nz)]
    first_sum = place(at, pieces, (tokens_here * nd) ** (-0.5))
    return join(at, [(low[0], low_up, low_down), (high[0], high_up, high_down)]), first_sum


def plain_body(inputs, first_factor, second_factor, cotangent):
    tokens_here = inputs.shape[0]
    in_width, local, out_width = first_factor.shape
    blocks = local * lax.axis_size("tensor")
    group = out_width // blocks
    block_grouped = inputs.reshape(tokens_here, local, in_width)
    split_first = first_factor.reshape(in_width, local, blocks, group)
    outgoing = jnp.einsum("tlk,kljg->jlgt", block_grouped, split_first, preferred_element_type=F32).astype(BF16)
    arrived = lax.all_to_all(outgoing, "tensor", split_axis=0, concat_axis=1, tiled=True)
    mixed = arrived.reshape(local, out_width, tokens_here)
    pre_act = jnp.einsum("lmt,mln->lnt", mixed, second_factor, preferred_element_type=F32)
    upstream = cotangent.reshape(local, out_width, tokens_here).astype(F32)
    pre_grad = (upstream * gelu_slope(pre_act)).astype(BF16)
    mixed_grad = jnp.einsum("lnt,mln->lmt", pre_grad, second_factor, preferred_element_type=F32).astype(BF16)
    returned = lax.all_to_all(
        mixed_grad.reshape(local, blocks, group, tokens_here), "tensor", split_axis=1, concat_axis=0, tiled=True
    )
    input_grad = jnp.einsum("jlgt,kljg->tlk", returned, split_first, preferred_element_type=F32)
    input_grad = input_grad.reshape(tokens_here, local * in_width).astype(BF16)
    factor = (tokens_here * lax.axis_size("dp")) ** (-0.5)
    first_term = jnp.einsum("tlk,jlgt->kljg", block_grouped, returned, preferred_element_type=F32)
    first_term = first_term.reshape(in_width, local, out_width)
    first_sum = lax.psum_scatter(first_term, "dp", scatter_dimension=0, tiled=True)
    return input_grad, first_sum * factor


def solution(mesh):
    nz, nd = mesh.shape["tensor"], mesh.shape["dp"]

    def run(inputs, first_factor, second_factor, cotangent):
        width, local, _ = first_factor.shape
        fits = nz == 4 and nd > 2 and local % 2 == 0 and width % (16 * nd) == 0 and nd & (nd - 1) == 0
        return (body if fits else plain_body)(inputs, first_factor, second_factor, cotangent)

    return jax.shard_map(
        run,
        mesh=mesh,
        in_specs=(
            P("dp", "tensor"),
            P(None, "tensor", None),
            P(None, "tensor", None),
            P("tensor", "dp"),
        ),
        out_specs=(P("dp", "tensor"), P("dp", "tensor", None)),
        check_vma=False,
    )
```

```python
import functools

import jax
import jax.numpy as jnp
from jax import lax
from jax.experimental import pallas as pl
from jax.experimental.pallas import tpu as pltpu
from jax.sharding import PartitionSpec as P

BF16 = jnp.bfloat16
F32 = jnp.float32


def dot(a, b, dims):
    return lax.dot_general(a, b, (dims, ((), ())), preferred_element_type=F32)


def gelu_slope(v):
    c = 0.7978845608028654
    v2 = v * v
    t = jnp.tanh(v * (c + (c * 0.044715) * v2))
    return 0.5 + 0.5 * t + (0.5 * v) * (1.0 - t * t) * (c + (3.0 * c * 0.044715) * v2)


LATE = pl.CostEstimate(flops=10**10, bytes_accessed=32 << 20, transcendentals=0)
VMEM = pl.BlockSpec(memory_space=pltpu.VMEM)
SMALL = pltpu.CompilerParams(vmem_limit_bytes=16 << 20)
FREE = pl.CostEstimate(flops=0, bytes_accessed=0, transcendentals=0)
SMEM = pl.BlockSpec(memory_space=pltpu.SMEM)


def on_chip(kernel, name, at, operands, shapes, stored=(), limit=16 << 20, cost=FREE, **more):
    held = [pltpu.with_memory_space_constraint(a, pltpu.VMEM) for a in operands]
    held += [pltpu.with_memory_space_constraint(a, pltpu.HBM) for a in stored]
    out = [pltpu.VMEM(shape, dtype) for shape, dtype in shapes]
    return pl.pallas_call(
        kernel,
        in_specs=[SMEM] + [VMEM] * len(operands) + [pl.BlockSpec(memory_space=pltpu.HBM)] * len(stored),
        out_specs=[VMEM] * len(out),
        out_shape=out,
        compiler_params=pltpu.CompilerParams(vmem_limit_bytes=limit),
        cost_estimate=cost,
        name=name,
        **more,
    )(at, *held)


def cut_kernel(nz, local, cols, kd, at_ref, f_ref, *outs):
    for r in range(1, nz):
        col = pl.multiple_of(lax.rem(at_ref[0] + nz - r, nz) * cols, cols)
        for b in range(local):
            outs[r - 1][b] = f_ref[:, b, pl.ds(col, cols)]


def cut(at, first_factor, nz, nd):
    width, local, out_width = first_factor.shape
    kd, cols = width // nd, out_width // nz
    return pl.pallas_call(
        functools.partial(cut_kernel, nz, local, cols, kd),
        grid_spec=pltpu.PrefetchScalarGridSpec(
            num_scalar_prefetch=1,
            grid=(1,),
            in_specs=[pl.BlockSpec((kd, local, out_width), lambda i, at_ref: (at_ref[1], 0, 0))],
            out_specs=[pl.BlockSpec((local, kd, cols), lambda i, at_ref: (0, 0, 0))] * (nz - 1),
        ),
        out_shape=[pltpu.VMEM((local, kd, cols), BF16)] * (nz - 1),
        compiler_params=SMALL,
        cost_estimate=FREE,
        name="cut",
    )(at, first_factor)


def own_kernel(local, at_ref, f_ref, later_ref, out):
    for b in range(local):
        out[b] = f_ref[:, b, :]


def own_columns(at, first_factor, earlier, nz):
    width, local, out_width = first_factor.shape
    cols = out_width // nz
    return pl.pallas_call(
        functools.partial(own_kernel, local),
        grid_spec=pltpu.PrefetchScalarGridSpec(
            num_scalar_prefetch=1,
            grid=(1,),
            in_specs=[pl.BlockSpec((width, local, cols), lambda i, at_ref: (0, 0, at_ref[0])), VMEM],
            out_specs=pl.BlockSpec((local, width, cols), lambda i, at_ref: (0, 0, 0)),
        ),
        out_shape=pltpu.VMEM((local, width, cols), BF16),
        compiler_params=SMALL,
        cost_estimate=FREE,
        name="own_columns",
    )(at, first_factor, pltpu.with_memory_space_constraint(earlier, pltpu.VMEM))


def turn_kernel(x_ref, later_ref, out):
    out[...] = x_ref[...].T


def turned(cotangent, earlier, tile=512):
    units, tokens = cotangent.shape
    return pl.pallas_call(
        turn_kernel,
        grid=(units // tile,),
        in_specs=[pl.BlockSpec((tile, tokens), lambda i: (i, 0)), VMEM],
        out_specs=pl.BlockSpec((tokens, tile), lambda i: (0, i)),
        out_shape=pltpu.VMEM((tokens, units), BF16),
        compiler_params=SMALL,
        cost_estimate=FREE,
        name="turned",
    )(cotangent, pltpu.with_memory_space_constraint(earlier, pltpu.VMEM))


def fetch_kernel(parts, at_ref, later_ref, a_hbm, out, arrived):
    copies = [pltpu.make_async_copy(a_hbm.at[j], out.at[j], arrived.at[j]) for j in range(parts)]
    for copy in copies:
        copy.start()
    for copy in copies:
        copy.wait()


def fetched(at, a, earlier):
    parts = a.shape[0]
    return on_chip(
        functools.partial(fetch_kernel, parts),
        "fetched",
        at,
        [earlier],
        [(a.shape, a.dtype)],
        stored=[a],
        scratch_shapes=[pltpu.SemaphoreType.DMA((parts,))],
    )[0]


def assemble_kernel(local, kd, orders, at_ref, own_ref, *refs):
    out = refs[-1]
    out[:local] = own_ref[...]
    core = jnp.bitwise_and(at_ref[1], 1)
    at = local
    for i, order in enumerate(orders):
        mine, other = refs[2 * i], refs[2 * i + 1]
        bits = len(order) + 1
        blocks = mine.shape[bits - 1]
        for d in range(1 << bits):
            place = tuple((d >> bit) & 1 for bit in reversed(order))
            for b in range(blocks):
                rows = jnp.where(core == (d & 1), mine[place + (b,)], other[place + (b,)])
                out[at + b, d * kd : (d + 1) * kd, :] = rows
        at += blocks


def layer_kernel(nz, local, width, cols, chunk, at_ref, *refs):
    x_refs = refs[:nz]
    f_ref, cot_ref, s_ref = refs[nz : nz + 3]
    *dx_refs, og_ref, mixed, back = refs[-(nz + 3) :]
    z = at_ref[0]
    group = cols // local
    rows, out_width = dx_refs[0].shape[0], mixed.shape[2]
    here = slice(chunk * rows, (chunk + 1) * rows)
    low = lax.broadcasted_iota(jnp.int32, (rows, 2 * group), 1) < group

    for r in range(nz):
        for b in range(0, local, 2):
            one = dot(x_refs[r][:, b * width : (b + 1) * width], f_ref[r * local + b], ((1,), (0,)))
            two = dot(x_refs[r][:, (b + 1) * width : (b + 2) * width], f_ref[r * local + b + 1], ((1,), (0,)))
            at = (r * local + b) * group
            for h in range(local // 2):
                p = one[:, 2 * h * group : (2 * h + 2) * group]
                q = two[:, 2 * h * group : (2 * h + 2) * group]
                mixed[2 * h, :, at : at + 2 * group] = jnp.where(low, p, pltpu.roll(q, group, 1)).astype(BF16)
                mixed[2 * h + 1, :, at : at + 2 * group] = jnp.where(low, pltpu.roll(p, group, 1), q).astype(BF16)

    planes = [lax.rem(z + r, nz) for r in range(nz)]

    for j in range(local):
        weight = jnp.concatenate(
            [s_ref[j, pl.ds(pl.multiple_of(p * cols, cols), cols), :] for p in planes], axis=0
        )
        pre_act = dot(mixed[j], weight, ((1,), (0,)))
        upstream = cot_ref[here, j * out_width : (j + 1) * out_width]
        pre_grad = (upstream.astype(F32) * gelu_slope(pre_act)).astype(BF16)
        back[j] = dot(pre_grad, weight, ((1,), (1,)))

    for r in range(nz):
        for b in range(0, local, 2):
            at = (r * local + b) * group
            one, two = [], []
            for h in range(local // 2):
                p = back[2 * h, :, at : at + 2 * group]
                q = back[2 * h + 1, :, at : at + 2 * group]
                one.append(jnp.where(low, p, pltpu.roll(q, group, 1)).astype(BF16))
                two.append(jnp.where(low, pltpu.roll(p, group, 1), q).astype(BF16))
            for i, part in ((b, one), (b + 1, two)):
                og = jnp.concatenate(part, axis=1)
                og_ref[r, :, i * cols : (i + 1) * cols] = og
                dx_refs[r][:, i * width : (i + 1) * width] = dot(
                    og, f_ref[r * local + i], ((1,), (1,))
                ).astype(dx_refs[r].dtype)


def layer(at, xs, first, second, cot, later, chunk, rows, nz, local, width, cols):
    out_width = second.shape[2]
    piece = (rows, local * width)
    return on_chip(
        functools.partial(layer_kernel, nz, local, width, cols, chunk),
        "layer",
        at,
        list(xs) + [first, cot, second, *later],
        [(piece, F32)] + [(piece, BF16)] * (nz - 1) + [((nz, rows, local * cols), BF16)],
        scratch_shapes=[
            pltpu.VMEM((local, rows, out_width), BF16),
            pltpu.VMEM((local, rows, out_width), F32),
        ],
    )


def grad_kernel(nz, parts, local, width, cols, nd, at_ref, *refs):
    x_refs, og_refs = refs[: parts * nz], refs[parts * nz : parts * (nz + 1)]
    give, keep = refs[-2:]
    me = at_ref[1]
    kd = width // nd
    for r in range(nz):
        for b in range(local):
            x = jnp.concatenate(
                [x_refs[c * nz + r][:, b * width : (b + 1) * width] for c in range(parts)], axis=0
            )
            og = jnp.concatenate([og_refs[c][r, :, b * cols : (b + 1) * cols] for c in range(parts)], axis=0)
            term = dot(x, og, ((0,), (0,))).astype(BF16)
            for d in range(0, nd, 2):
                to = lax.div(jnp.bitwise_xor(me, d), 2)
                low, high = term[d * kd : (d + 1) * kd], term[(d + 1) * kd : (d + 2) * kd]
                odd = jnp.bitwise_and(me, 1) == 1
                keep[to, r * local + b] = jnp.where(odd, high, low)
                give[to, r * local + b] = jnp.where(odd, low, high)


def first_grad_terms(at, xs, ogs, later, nz, local, width, cols, nd):
    shape = (nd // 2, nz * local, width // nd, cols)
    return on_chip(
        functools.partial(grad_kernel, nz, len(ogs), local, width, cols, nd),
        "first_grad_terms",
        at,
        [a for x in xs for a in x] + list(ogs) + list(later),
        [(shape, BF16)] * 2,
    )


def sums_kernel(plan, at_ref, *refs):
    used = 0
    for i, has_got in enumerate(plan):
        total = refs[used][...]
        if has_got:
            total = (total.astype(F32) + refs[used + 1][...].astype(F32)).astype(BF16)
        used += 1 + has_got
        refs[i - len(plan)][...] = total


def sums(at, pairs, *earlier):
    return on_chip(
        functools.partial(sums_kernel, [got is not None for _, got in pairs]),
        "sums",
        at,
        [a for pair in pairs for a in pair if a is not None] + list(earlier),
        [(part.shape, BF16) for part, _ in pairs],
        cost=LATE,
    )


def after(at, values, *earlier, stored=()):
    return on_chip(
        functools.partial(sums_kernel, [False] * len(values)),
        "after",
        at,
        list(values) + list(earlier),
        [(v.shape, v.dtype) for v in values],
        stored=stored,
        cost=LATE,
    )


def mark_kernel(at_ref, *refs):
    refs[-1][...] = jnp.zeros_like(refs[-1])


def mark(at, values):
    held = [pltpu.with_memory_space_constraint(a, pltpu.VMEM) for a in values]
    return pl.pallas_call(
        mark_kernel,
        in_specs=[SMEM] + [VMEM] * len(held),
        out_specs=VMEM,
        out_shape=pltpu.VMEM((8, 128), F32),
        compiler_params=SMALL,
        cost_estimate=LATE,
        name="mark",
    )(at, *held)


def pass_kernel(at_ref, first_ref, *refs):
    inputs_hbm, first_out, second_out, arrived = refs[-4:]
    rows = second_out.shape[0]
    copy = pltpu.make_async_copy(inputs_hbm.at[pl.ds(rows, rows)], second_out, arrived)
    copy.start()
    first_out[...] = first_ref[...]
    copy.wait()


def halved_kernel(count, at_ref, *refs):
    low, high = refs[-2:]
    half, size = low.shape[0], refs[0].shape[0]
    for i in range(count):
        for b in range(size):
            at = i * size + b
            (low if at < half else high)[at % half] = refs[i][b]


def halved(at, blocks, *earlier):
    size, kd, cols = blocks[0].shape
    shape = (len(blocks) * size // 2, kd, cols)
    return on_chip(
        functools.partial(halved_kernel, len(blocks)), "halved", at, list(blocks) + list(earlier), [(shape, BF16)] * 2
    )


def join_kernel(at_ref, *refs):
    out = refs[-1]
    rows = refs[0].shape[0]
    for c in range(2):
        own, up, down = [ref[...].astype(F32) for ref in refs[3 * c : 3 * c + 3]]
        out[c * rows : (c + 1) * rows] = (own + up + down).astype(BF16)


def join(at, halves):
    late = mark(at, [halves[0][1], halves[1][1]])
    held = [pltpu.with_memory_space_constraint(a, pltpu.VMEM) for half in halves for a in half] + [late]
    rows, width = held[0].shape
    return pl.pallas_call(
        join_kernel,
        in_specs=[SMEM] + [VMEM] * len(held),
        out_specs=VMEM,
        out_shape=jax.ShapeDtypeStruct((rows * 2, width), BF16),
        compiler_params=SMALL,
        cost_estimate=FREE,
        name="join",
    )(at, *held)


def place_kernel(nz, local, cols, factor, at_ref, *refs):
    out = refs[-1]
    for r in range(nz):
        at = pl.multiple_of(lax.rem(at_ref[0] + nz - r, nz) * cols, cols)
        for b in range(local):
            out[:, b, pl.ds(at, cols)] = refs[r][b].astype(F32) * factor


def place(at, pieces, factor):
    nz = len(pieces)
    local, kd, cols = pieces[0].shape
    held = [pltpu.with_memory_space_constraint(a, pltpu.VMEM) for a in pieces]
    return pl.pallas_call(
        functools.partial(place_kernel, nz, local, cols, factor),
        in_specs=[SMEM] + [VMEM] * nz,
        out_specs=VMEM,
        out_shape=jax.ShapeDtypeStruct((kd, local, nz * cols), F32),
        compiler_params=SMALL,
        cost_estimate=LATE,
        name="place",
    )(at, *held)


def swap(bit, nd):
    return [(i, i ^ (1 << bit)) for i in range(nd)]


def ring_step(value, step, nz):
    return lax.ppermute(value, "tensor", [(i, (i + step) % nz) for i in range(nz)])


def double_over_dp(part, bit, d, nd):
    got = lax.ppermute(part, "dp", swap(bit, nd))
    upper = (d >> bit) & 1 == 1
    return jnp.stack([jnp.where(upper, got, part), jnp.where(upper, part, got)])


def body(inputs, first_factor, second_factor, cotangent):
    nz, nd = lax.axis_size("tensor"), lax.axis_size("dp")
    z, d = lax.axis_index("tensor"), lax.axis_index("dp")
    at = jnp.stack([z, d]).astype(jnp.int32)
    tokens_here = inputs.shape[0]
    width, local, out_width = first_factor.shape
    cols = out_width // nz
    kd = width // nd
    rows = tokens_here // 2
    bits = nd.bit_length() - 1
    orders = [list(range(1, bits)), list(range(bits - 1, 0, -1))]

    xs = [[inputs[:rows]] + [None] * (nz - 1), [None] * nz]
    xs[0][3] = ring_step(xs[0][0], 1, nz)
    xs[0][1] = ring_step(xs[0][0], -1, nz)
    second = second_factor.transpose(1, 0, 2)
    sends = cut(at, first_factor, nz, nd)
    got = [ring_step(sends[r - 1], -r, nz) for r in range(1, nz)]
    xs[0][3], xs[1][0] = on_chip(
        pass_kernel,
        "pass_on",
        at,
        [xs[0][3], xs[0][1], *got],
        [(xs[0][0].shape, BF16)] * 2,
        stored=[second, inputs],
        cost=LATE,
        scratch_shapes=[pltpu.SemaphoreType.DMA],
    )
    xs[0][2] = ring_step(xs[0][3], 1, nz)
    xs[1][1] = ring_step(xs[1][0], -1, nz)
    xs[1][3] = ring_step(xs[1][0], 1, nz)

    others = halved(at, got, xs[0][3])
    for k in range(bits - 1):
        others = [double_over_dp(o, order[k], d, nd) for o, order in zip(others, orders)]
        if k == 0:
            own = own_columns(at, first_factor, others[0], nz)
    cot = turned(cotangent, others[1])
    pieces = []
    for o in others:
        pieces += [o, lax.ppermute(o, "dp", swap(0, nd))]
    first = on_chip(
        functools.partial(assemble_kernel, local, kd, orders),
        "assemble",
        at,
        [own] + pieces,
        [((nz * local, width, cols), BF16)],
    )[0]
    second = fetched(at, second, others[0])
    (xs[1][1],) = after(at, [xs[1][1]], xs[0][2], xs[1][3], own, cot, second)
    xs[1][2] = ring_step(xs[1][1], -1, nz)

    low = layer(at, xs[0], first, second, cot, [xs[1][1]], 0, rows, nz, local, width, cols)
    low_far = ring_step(low[2], 1, nz)
    low_down = ring_step(low[3], -1, nz)
    high = layer(at, xs[1], first, second, cot, [], 1, rows, nz, local, width, cols)
    high_far = ring_step(high[2], -1, nz)
    high_up = ring_step(high[1], 1, nz)
    give, keep = first_grad_terms(at, xs, [low[nz], high[nz]], [], nz, local, width, cols, nd)
    sent = sums(at, [(low[1], low_far)], low_down, give)
    low_up = ring_step(sent[0], 1, nz)

    got = lax.ppermute(give, "dp", swap(0, nd))
    keep = keep.reshape([2] * (bits - 1) + list(keep.shape[1:]))
    got = got.reshape(keep.shape)
    half = nz * local // 2
    totals = []
    for i in range(2):
        cut_half = lambda a: a[(slice(None),) * (bits - 1) + (slice(i * half, (i + 1) * half),)]
        totals.append(cut_half(keep).astype(F32) + cut_half(got).astype(F32))
    left = [list(range(bits - 1, 0, -1)) for _ in range(2)]
    for k in range(bits - 1):
        give = []
        for i in range(2):
            axis = left[i].index(orders[i][k])
            left[i].remove(orders[i][k])
            pick = lambda n: lax.index_in_dim(totals[i], n, axis, keepdims=False)
            give.append(pick(1).astype(BF16))
            totals[i] = pick(0)
        if k == 0:
            sent = sums(at, [(high[3], high_far)], *give)
        for i in range(2):
            totals[i] = totals[i] + lax.ppermute(give[i], "dp", swap(orders[i][k], nd)).astype(F32)
    high_down = ring_step(sent[0], -1, nz)
    blocks = jnp.concatenate(totals, axis=0).reshape(nz, local, kd, cols)
    give = [blocks[r].astype(BF16) for r in range(1, nz)]
    pieces = [blocks[0]] + [ring_step(give[r - 1], r, nz) for r in range(1, nz)]
    first_sum = place(at, pieces, (tokens_here * nd) ** (-0.5))
    return join(at, [(low[0], low_up, low_down), (high[0], high_up, high_down)]), first_sum


def plain_body(inputs, first_factor, second_factor, cotangent):
    tokens_here = inputs.shape[0]
    in_width, local, out_width = first_factor.shape
    blocks = local * lax.axis_size("tensor")
    group = out_width // blocks
    block_grouped = inputs.reshape(tokens_here, local, in_width)
    split_first = first_factor.reshape(in_width, local, blocks, group)
    outgoing = jnp.einsum("tlk,kljg->jlgt", block_grouped, split_first, preferred_element_type=F32).astype(BF16)
    arrived = lax.all_to_all(outgoing, "tensor", split_axis=0, concat_axis=1, tiled=True)
    mixed = arrived.reshape(local, out_width, tokens_here)
    pre_act = jnp.einsum("lmt,mln->lnt", mixed, second_factor, preferred_element_type=F32)
    upstream = cotangent.reshape(local, out_width, tokens_here).astype(F32)
    pre_grad = (upstream * gelu_slope(pre_act)).astype(BF16)
    mixed_grad = jnp.einsum("lnt,mln->lmt", pre_grad, second_factor, preferred_element_type=F32).astype(BF16)
    returned = lax.all_to_all(
        mixed_grad.reshape(local, blocks, group, tokens_here), "tensor", split_axis=1, concat_axis=0, tiled=True
    )
    input_grad = jnp.einsum("jlgt,kljg->tlk", returned, split_first, preferred_element_type=F32)
    input_grad = input_grad.reshape(tokens_here, local * in_width).astype(BF16)
    factor = (tokens_here * lax.axis_size("dp")) ** (-0.5)
    first_term = jnp.einsum("tlk,jlgt->kljg", block_grouped, returned, preferred_element_type=F32)
    first_term = first_term.reshape(in_width, local, out_width)
    first_sum = lax.psum_scatter(first_term, "dp", scatter_dimension=0, tiled=True)
    return input_grad, first_sum * factor


def solution(mesh):
    nz, nd = mesh.shape["tensor"], mesh.shape["dp"]

    def run(inputs, first_factor, second_factor, cotangent):
        width, local, _ = first_factor.shape
        fits = nz == 4 and nd > 2 and local % 2 == 0 and width % (16 * nd) == 0 and nd & (nd - 1) == 0
        return (body if fits else plain_body)(inputs, first_factor, second_factor, cotangent)

    return jax.shard_map(
        run,
        mesh=mesh,
        in_specs=(
            P("dp", "tensor"),
            P(None, "tensor", None),
            P(None, "tensor", None),
            P("tensor", "dp"),
        ),
        out_specs=(P("dp", "tensor"), P("dp", "tensor", None)),
        check_vma=False,
    )
```
